32 devices in a mesh: scen: 2 (over y), gx: 4 (over z), gy: 4 (over x, core).
Axes of the slice: x: 2, y: 2, z: 4, core: 2. Of those that a mesh axis runs over, the one named last changes fastest.
Arguments:
- ocean_eta: float32 [512, 512], P(('scen', 'gx'), 'gy'), parts along dimension 0, may hold values from -1 to 1
- ocean_mx: float32 [512, 512], P(('scen', 'gx'), 'gy'), parts along dimension 0, may hold values from -1.5 to 1.5
- ocean_ny: float32 [512, 512], P(('scen', 'gx'), 'gy'), parts along dimension 0, may hold values from -1.5 to 1.5
- ocean_depth: float32 [512, 512], P(('scen', 'gx'), 'gy'), parts along dimension 0, may hold values from 0.1 to 2
- ocean_class: int32 [512, 512], P(('scen', 'gx'), 'gy'), parts along dimension 0, may hold values from 0 to 5
- manning: float32 [6], replicated, may hold values from 0.05 to 0.8
- fine_eta: float32 [1536, 1536], P(('scen', 'gx'), 'gy'), parts along dimension 0, may hold values from -1 to 1
- fine_qx: float32 [1536, 1536], P(('scen', 'gx'), 'gy'), parts along dimension 0, may hold values from -1 to 1
- fine_qy: float32 [1536, 1536], P(('scen', 'gx'), 'gy'), parts along dimension 0, may hold values from -1 to 1
- fine_depth: float32 [1536, 1536], P(('scen', 'gx'), 'gy'), parts along dimension 0, may hold values from -0.2 to 1
- fine_wet: int32 [1536, 1536], P(('scen', 'gx'), 'gy'), parts along dimension 0, may hold values 0 or 1
- fine_class: int32 [1536, 1536], P(('scen', 'gx'), 'gy'), parts along dimension 0, may hold values from 0 to 5
- fine_offset: int32 [4], P('scen'), parts along dimension 0, may hold values from 1 to 63, as said below
Outputs:
- new_ocean_eta: float32 [512, 512], P(('scen', 'gx'), 'gy'), parts along dimension 0
- new_ocean_mx: float32 [512, 512], P(('scen', 'gx'), 'gy'), parts along dimension 0
- new_ocean_ny: float32 [512, 512], P(('scen', 'gx'), 'gy'), parts along dimension 0
- new_fine_eta: float32 [1536, 1536], P(('scen', 'gx'), 'gy'), parts along dimension 0
- new_fine_qx: float32 [1536, 1536], P(('scen', 'gx'), 'gy'), parts along dimension 0
- new_fine_qy: float32 [1536, 1536], P(('scen', 'gx'), 'gy'), parts along dimension 0
The draws below stay inside these ranges and needn't reach their ends.
There are 2 independent parts, one for each index of `scen`. The reference program is written for one: setup_inputs(seed, part) draws one part's arguments, and reference() takes and returns one part's arrays. A program takes and returns all parts, laid end to end along the dimension named above; an argument that names none is the same for every part. Nothing has to cross between parts.
Inputs may be any that keep to these rules, and one draw needn't show every extreme that they name: `fine_offset`: one coastal grid has offset 1 and another has offset 64 - 1.
All inputs are finite; a program needn't handle non-finite values. No bound on the sum of `fine_wet` on one device may be relied on, other than what follows from the above.
Results may differ from the reference program's by a relative error of at most 0.0003.
Values sent between devices are 32-bit elements; how exact they have to be, the bound alone decides.
No kernel may reach another device: no remote copies, remote signals or barrier semaphores. Data moves between devices by JAX's collectives and lax.ppermute only.
A program may use at most 64 MiB of HBM per device.

```python
import math
import jax
import jax.numpy as jnp
from jax import lax

CX = 64
R = 3
ITERS = 4
NCLASS = 6
FSTEPS = 12
GB = 2
FINE = 2
NX = 256
NY = 512
FXT = 768
FYT = 1536


def draw_fine_offset(key, part):
    key = jax.random.fold_in(key, 11)
    first_key, second_key = jax.random.split(key)
    values = jax.random.randint(first_key, (FINE,), 1, CX)
    lower = jax.random.randint(second_key, (), 0, FINE)
    upper = (lower + 1) % FINE
    positions = jnp.arange(FINE)
    values = jnp.where(positions == lower, 1, values)
    values = jnp.where(positions == upper, CX - 1, values)
    return values.astype(jnp.int32)


def set_ends(drawn, rng, least, top_value):
    spot = [jax.random.randint(jax.random.fold_in(rng, axis), (), 0, length) for axis, length in enumerate(drawn.shape)]
    longest = drawn.shape.index(max(drawn.shape))
    beside = spot[:longest] + [(spot[longest] + 1) % drawn.shape[longest]] + spot[longest + 1:]
    return drawn.at[tuple(spot)].set(least).at[tuple(beside)].set(top_value)


def steps_of(rng, shape, pieces, smallest, top_value):
    def one(position, blocks):
        steps = jax.random.uniform(jax.random.fold_in(jax.random.fold_in(rng, 6), position), (blocks,), jnp.float32, smallest / len(pieces), top_value / len(pieces))
        return jnp.repeat(jnp.exp(steps), shape[position] // blocks).reshape((-1,) + (1,) * (len(shape) - position - 1))

    loudness = one(*pieces[0])
    for cut in pieces[1:]:
        loudness = loudness * one(*cut)
    return loudness


def gaussian(stream_key, shape, width, limit, pieces=(), kind=jnp.bfloat16):
    entries = jax.random.normal(stream_key, shape, jnp.float32) * width
    if len(pieces) > 0:
        entries = steps_of(stream_key, shape, pieces, -0.22, 0.18) * entries
    return jnp.clip(entries, min=-limit, max=limit).astype(kind)


def setup_inputs(seed: int = 0, part: int = 0) -> dict:
    keys = jax.random.split(jax.random.key(seed), 14)
    part_keys = jax.random.split(jax.random.fold_in(keys[13], part), 14)
    ocean_eta = gaussian(part_keys[0], (NX, NY), 0.2, 1.0, ((0, 4), (1, 4)), jnp.float32)
    ocean_mx = gaussian(part_keys[1], (NX, NY), 0.3, 1.5, ((0, 4), (1, 4)), jnp.float32)
    ocean_ny = gaussian(part_keys[2], (NX, NY), 0.3, 1.5, ((0, 4), (1, 4)), jnp.float32)
    ocean_depth = jnp.clip(jnp.exp(math.log(2.0) - 2.9957323 * jax.random.uniform(part_keys[3], (NX, NY), jnp.float32) ** steps_of(part_keys[3], (NX, NY), ((0, 4), (1, 4)), -0.2, 0.2)), 0.1, 2.0)
    ocean_class = set_ends(jax.random.randint(part_keys[4], (NX, NY), 0, NCLASS), jax.random.fold_in(part_keys[4], 1), 0, NCLASS - 1).astype(jnp.int32)
    manning = jnp.clip(jnp.exp(jax.random.uniform(keys[5], (NCLASS,), jnp.float32, math.log(0.05), math.log(0.8))), 0.05, 0.8)
    fine_eta = gaussian(part_keys[6], (FXT, FYT), 0.2, 1.0, ((0, 4), (1, 4)), jnp.float32)
    fine_qx = gaussian(part_keys[7], (FXT, FYT), 0.2, 1.0, ((0, 4), (1, 4)), jnp.float32)
    fine_qy = gaussian(part_keys[8], (FXT, FYT), 0.2, 1.0, ((0, 4), (1, 4)), jnp.float32)
    fine_depth = jnp.clip(-0.2 + 1.2 * jax.random.uniform(part_keys[9], (FXT, FYT), jnp.float32) ** steps_of(part_keys[9], (FXT, FYT), ((0, 4), (1, 4)), -0.2, 0.2), -0.2, 1.0)
    fine_wet = set_ends((jax.random.randint(part_keys[10], (FXT, FYT), 0, 4) < 3).astype(jnp.int32), jax.random.fold_in(part_keys[10], 1), 0, 1)
    fine_class = set_ends(jax.random.randint(part_keys[11], (FXT, FYT), 0, NCLASS), jax.random.fold_in(part_keys[11], 1), 0, NCLASS - 1).astype(jnp.int32)
    fine_offset = draw_fine_offset(jax.random.fold_in(jax.random.fold_in(keys[13], part), 71), part)
    return dict(ocean_eta=ocean_eta, ocean_mx=ocean_mx, ocean_ny=ocean_ny, ocean_depth=ocean_depth, ocean_class=ocean_class, manning=manning, fine_eta=fine_eta, fine_qx=fine_qx, fine_qy=fine_qy, fine_depth=fine_depth, fine_wet=fine_wet, fine_class=fine_class, fine_offset=fine_offset)


COURANT = 0.45
FLOOR = 0.25
EXPO = 7.0 / 3.0


def friction_of(classes, table):
    result = jnp.zeros(classes.shape, jnp.float32)
    for level_id in range(table.shape[0]):
        result = result + jnp.where(classes == level_id, table[level_id], jnp.float32(0.0))
    return result


def momentum(flux, eta, eta_next, depth, depth_next, kfric, kfric_next, openness):
    total = 0.5 * (jnp.maximum(depth + eta, 0.0) + jnp.maximum(depth_next + eta_next, 0.0))
    drag = 1.0 + COURANT * 0.5 * (kfric + kfric_next) * jnp.abs(flux) / jnp.power(jnp.maximum(total, FLOOR), EXPO)
    return openness * (flux - COURANT * total * (eta_next - eta)) / drag


def level(eta, flux_x, flux_y, west_row, south_col):
    flux_west = jnp.concatenate([west_row, flux_x[:-1]], 0)
    flux_south = jnp.concatenate([south_col, flux_y[:, :-1]], 1)
    return eta - COURANT * (flux_x - flux_west + flux_y - flux_south)


def flows(eta, flux_x, flux_y, depth, kfric, north_rows, east_cols, open_x, open_y):
    eta_n0 = jnp.concatenate([eta[1:], north_rows[0]], 0)
    depth_n0 = jnp.concatenate([depth[1:], north_rows[1]], 0)
    kfric_n0 = jnp.concatenate([kfric[1:], north_rows[2]], 0)
    eta_n1 = jnp.concatenate([eta[:, 1:], east_cols[0]], 1)
    depth_n1 = jnp.concatenate([depth[:, 1:], east_cols[1]], 1)
    kfric_n1 = jnp.concatenate([kfric[:, 1:], east_cols[2]], 1)
    new_x = momentum(flux_x, eta, eta_n0, depth, depth_n0, kfric, kfric_n0, open_x)
    new_y = momentum(flux_y, eta, eta_n1, depth, depth_n1, kfric, kfric_n1, open_y)
    return new_x, new_y


def reference(ocean_eta, ocean_mx, ocean_ny, ocean_depth, ocean_class, manning, fine_eta, fine_qx, fine_qy, fine_depth, fine_wet, fine_class, fine_offset):
    kfric = friction_of(ocean_class, manning)
    open_x = (jnp.arange(NX, dtype=jnp.int32) < NX - 1).astype(jnp.float32)[:, None]
    open_y = (jnp.arange(NY, dtype=jnp.int32) < NY - 1).astype(jnp.float32)[None, :]
    zero_row = jnp.zeros((1, NY), jnp.float32)
    zero_col = jnp.zeros((NX, 1), jnp.float32)
    eta, flux_x, flux_y = ocean_eta, ocean_mx, ocean_ny
    for step in range(ITERS):
        eta = level(eta, flux_x, flux_y, zero_row, zero_col)
        flux_x, flux_y = flows(eta, flux_x, flux_y, ocean_depth, kfric, (zero_row, zero_row, zero_row), (zero_col, zero_col, zero_col), open_x, open_y)

    band = GB * CX
    span = GB * R * CX

    def one_grid(grid):
        first = (grid * span).astype(jnp.int32)

        def take(field):
            return lax.dynamic_slice_in_dim(field, first, span, 0)

        offset = fine_offset[grid]
        top = (grid * band + offset - 1).astype(jnp.int32)
        west_src = lax.dynamic_slice_in_dim(ocean_mx, top, 1, 0)
        bottom = ((grid + 1) * band - 1).astype(jnp.int32)
        east_src = lax.dynamic_slice_in_dim(ocean_mx, bottom, 1, 0)
        wet = take(fine_wet).astype(jnp.float32)
        depth = take(fine_depth)
        fkfric = friction_of(take(fine_class), manning)
        west = jnp.repeat(west_src, R, axis=1) * wet[:1]
        east = jnp.repeat(east_src, R, axis=1) * wet[-1:]
        frow = jnp.zeros((1, FYT), jnp.float32)
        fcol = jnp.zeros((span, 1), jnp.float32)
        face_x = wet * jnp.concatenate([wet[1:], frow], 0)
        face_y = wet * jnp.concatenate([wet[:, 1:], fcol], 1)
        feta, fqx, fqy = take(fine_eta), take(fine_qx), take(fine_qy)
        for step in range(FSTEPS):
            feta = level(feta, fqx, fqy, west, fcol)
            fqx, fqy = flows(feta, fqx, fqy, depth, fkfric, (frow, frow, frow), (fcol, fcol, fcol), face_x, face_y)
            fqx = jnp.concatenate([fqx[:-1], east], 0)
        means = jnp.mean(feta.reshape(band, R, NY, R), axis=(1, 3))
        return feta, fqx, fqy, means

    feta, fqx, fqy, means = lax.map(one_grid, jnp.arange(FINE, dtype=jnp.int32))
    canvas = jnp.concatenate([eta, jnp.zeros((band, NY), jnp.float32)], 0)

    def place(grid, field):
        start = (grid * band + fine_offset[grid]).astype(jnp.int32)
        return lax.dynamic_update_slice_in_dim(field, means[grid], start, 0)

    canvas = lax.fori_loop(0, FINE, place, canvas)
    return canvas[:NX], flux_x, flux_y, feta.reshape(FXT, FYT), fqx.reshape(FXT, FYT), fqy.reshape(FXT, FYT)
```

```python
import functools

import jax
import jax.numpy as jnp
from jax import lax
from jax.experimental import pallas as pl
from jax.experimental.pallas import tpu as pltpu
from jax.sharding import PartitionSpec as P

R = 3
ITERS = 4
FSTEPS = R * ITERS
COURANT = 0.45
FLOOR = 0.25
SA = COURANT**2 / 2
SB = COURANT**3 / 2
POWER = -7.0 / 3.0
TFLOOR = 2 * SA * FLOOR
KSCALE = 0.5 * COURANT * (2 * SA) ** (7.0 / 3.0) / SB
CLOSED = 3.0e38
LANES = 128
HALO = 16
OLANE = 6 * 16
VMEM = pl.BlockSpec(memory_space=pltpu.VMEM)
SMEM = pl.BlockSpec(memory_space=pltpu.SMEM)
F32 = jnp.float32


def swap_even(value, axis):
    count = lax.axis_size(axis)
    return lax.ppermute(value, axis, [(i, i ^ 1) for i in range(count) if i ^ 1 < count])


def swap_odd(value, axis):
    count = lax.axis_size(axis)
    pairs = [(i, ((i + 1) ^ 1) - 1) for i in range(1, count)]
    return lax.ppermute(value, axis, [(a, b) for a, b in pairs if b < count])


def friction(classes, table):
    result = jnp.full(classes.shape, table[0], F32)
    for level_id in range(1, table.shape[0]):
        result = jnp.where(classes == level_id, table[level_id], result)
    return result


def fine_fields(refs, rows, cols, table):
    eta, qx, qy, depth, wet, classes = refs
    return (
        eta[rows, cols] * SA,
        qx[rows, cols] * SB,
        qy[rows, cols] * SB,
        depth[rows, cols] * SA,
        friction(classes[rows, cols], table),
        wet[rows, cols].astype(F32),
    )


def ocean_fields(refs, rows, cols, table):
    eta, mx, ny, depth, classes = refs
    return (
        eta[rows, cols] * SA,
        mx[rows, cols] * SB,
        ny[rows, cols] * SB,
        depth[rows, cols] * SA,
        friction(classes[rows, cols], table),
    )


def roll_to(value, start, target):
    return pltpu.roll(value, (target - start) % LANES, 1)


def pack_columns_kernel(fine_cols, *refs):
    table, fine, ocean, (even_out, odd_out) = refs[0], refs[1:7], refs[7:12], refs[12:14]
    rows, cols = fine[0].shape
    ocean_rows = ocean[0].shape[0]
    lane = lax.broadcasted_iota(jnp.int32, (8, LANES), 1)
    is_even = lax.rem(lax.axis_index("gy"), 2) == 0
    for r in range(rows // 8):
        row = pl.ds(8 * r, 8)
        west = jnp.zeros((8, LANES), F32)
        east = jnp.zeros((8, LANES), F32)
        if 8 * r < ocean_rows:
            for j, value in enumerate(ocean_fields(ocean, row, pl.ds(0, LANES), table)):
                west = jnp.where(lane >= OLANE + 4 * j, roll_to(value, 0, OLANE + 4 * j), west)
                east = jnp.where(lane >= OLANE + 4 * j, roll_to(value, LANES - 4, OLANE + 4 * j), east)
        first = fine_fields(fine, row, pl.ds(0, LANES), table)
        last = fine_fields(fine, row, pl.ds(cols - LANES, LANES), table)
        for f in range(5, -1, -1):
            west = jnp.where(lane < 16 * f + 16, roll_to(first[f], 0, 16 * f), west)
            east = jnp.where(lane < 16 * f + 16, roll_to(last[f], LANES - 16, 16 * f), east)
        even_out[row, :] = jnp.where(is_even, east, west)
        odd_out[row, :] = jnp.where(is_even, west, east)


def pack_rows_kernel(pairs_only, *refs):
    table, fine, ocean, (gy_even, gy_odd) = refs[0], refs[1:7], refs[7:12], refs[12:14]
    even_out, odd_out = refs[14:16]
    rows, cols = fine[0].shape
    tiles = cols // LANES
    ocean_rows = ocean[0].shape[0]
    is_even = lax.rem(lax.axis_index("gx"), 2) == 0
    fine_rows = (6 * tiles + 2) * HALO

    def choose(base, with_fine, out, low):
        at = 0
        if with_fine:
            for f_tile in range(tiles):
                cols_at = pl.ds(f_tile * LANES, LANES)
                for half in range(HALO // 8):
                    top = fine_fields(fine, pl.ds(8 * half, 8), cols_at, table)
                    bottom = fine_fields(fine, pl.ds(rows - HALO + 8 * half, 8), cols_at, table)
                    for f in range(6):
                        place = (f * tiles + f_tile) * HALO + 8 * half
                        out[pl.ds(place, 8), :] = jnp.where(low, bottom[f], top[f])
            for k, src in enumerate((gy_even, gy_odd)):
                for half in range(HALO // 8):
                    place = (6 * tiles + k) * HALO + 8 * half
                    out[pl.ds(place, 8), :] = jnp.where(
                        low, src[pl.ds(rows - HALO + 8 * half, 8), :], src[pl.ds(8 * half, 8), :]
                    )
            at = fine_rows
        top = ocean_fields(ocean, pl.ds(0, 8), pl.ds(0, LANES), table)
        bottom = ocean_fields(ocean, pl.ds(ocean_rows - 8, 8), pl.ds(0, LANES), table)
        for j in range(5):
            out[pl.ds(at + 8 * j, 8), :] = jnp.where(low, bottom[j], top[j])
        for k, src in enumerate((gy_even, gy_odd)):
            out[pl.ds(at + 8 * (5 + k), 8), :] = jnp.where(
                low, src[pl.ds(ocean_rows - 8, 8), :], src[pl.ds(0, 8), :]
            )

    choose(0, True, even_out, is_even)
    choose(0, not pairs_only, odd_out, jnp.logical_not(is_even))


def lane_next(values):
    lane = lax.broadcasted_iota(jnp.int32, values[0].shape, 1)
    rolled = [pltpu.roll(v, LANES - 1, 1) for v in values]
    if len(values) == 1:
        return rolled
    return [jnp.where(lane == LANES - 1, rolled[(t + 1) % len(values)], rolled[t]) for t in range(len(values))]


def lane_prev(values):
    lane = lax.broadcasted_iota(jnp.int32, values[0].shape, 1)
    rolled = [pltpu.roll(v, 1, 1) for v in values]
    if len(values) == 1:
        return rolled
    return [jnp.where(lane == 0, rolled[t - 1], rolled[t]) for t in range(len(values))]


def new_flux(flux, eta, eta_next, wet, wet_next, opened, drag):
    total = wet + wet_next
    power = jnp.exp2(POWER * jnp.log2(jnp.maximum(total, TFLOOR)))
    denom = opened + (drag * jnp.abs(flux)) * power
    return (flux - total * (eta_next - eta)) / denom


def prepare_faces(tiles, n, kf, wf, kx, ky, ox, oy, open_x=None, open_y=None):
    for t in range(tiles):
        wrap = pl.ds(8 + 8 * n, 8)
        kf[t, wrap, :] = kf[t, pl.ds(8, 8), :]
        if wf is not None:
            wf[t, wrap, :] = wf[t, pl.ds(8, 8), :]
    for r in range(n):
        here, after = pl.ds(8 + 8 * r, 8), pl.ds(9 + 8 * r, 8)
        k = [kf[t, here, :] for t in range(tiles)]
        k_next = lane_next(k)
        if wf is not None:
            w = [wf[t, here, :] for t in range(tiles)]
            w_next = lane_next(w)
        for t in range(tiles):
            kx[t, here, :] = KSCALE * (k[t] + kf[t, after, :])
            ky[t, here, :] = KSCALE * (k[t] + k_next[t])
            if wf is not None:
                ox[t, here, :] = jnp.where(w[t] * wf[t, after, :] > 0.5, 1.0, CLOSED)
                oy[t, here, :] = jnp.where(w[t] * w_next[t] > 0.5, 1.0, CLOSED)


def level_pass(tiles, n, e, g, x, y, d):
    for r in range(n):
        here, before = pl.ds(8 + 8 * r, 8), pl.ds(7 + 8 * r, 8)
        south = [y[t, here, :] for t in range(tiles)]
        south_prev = lane_prev(south)
        for t in range(tiles):
            flow = (x[t, here, :] - x[t, before, :]) + (south[t] - south_prev[t])
            eta = e[t, here, :] - flow
            wet = jnp.maximum(d[t, here, :] + eta, 0.0)
            e[t, here, :] = eta
            g[t, here, :] = wet
            if r == 0:
                e[t, pl.ds(8 + 8 * n, 8), :] = eta
                g[t, pl.ds(8 + 8 * n, 8), :] = wet


def flux_pass(tiles, n, e, g, x, y, kx, ky, ox, oy, fix):
    for r in range(n):
        here, after = pl.ds(8 + 8 * r, 8), pl.ds(9 + 8 * r, 8)
        eta = [e[t, here, :] for t in range(tiles)]
        wet = [g[t, here, :] for t in range(tiles)]
        eta_next, wet_next = lane_next(eta), lane_next(wet)
        for t in range(tiles):
            fx = new_flux(
                x[t, here, :], eta[t], e[t, after, :], wet[t], g[t, after, :], ox[t, here, :], kx[t, here, :]
            )
            fx = fix(r, t, fx)
            x[t, here, :] = fx
            if r == n - 1:
                x[t, pl.ds(0, 8), :] = fx
            y[t, here, :] = new_flux(
                y[t, here, :], eta[t], eta_next[t], wet[t], wet_next[t], oy[t, here, :], ky[t, here, :]
            )


def dot(a, b):
    return lax.dot_general(
        a, b, (((1,), (0,)), ((), ())), precision=lax.Precision.HIGHEST, preferred_element_type=F32
    )


def iota(shape, dim):
    return lax.broadcasted_iota(jnp.int32, shape, dim)


def place_of(block_size):
    gx = lax.axis_index("gx")
    slot = lax.rem(gx, block_size)
    return gx, lax.div(gx, block_size), slot == 0, slot == block_size - 1


def fine_kernel(block_size, *refs):
    table, offsets, fine, ocean_mx = refs[0], refs[1], refs[2:8], refs[8]
    gy_even, gy_odd, gx_even, gx_odd = refs[9:13]
    out_eta, out_x, out_y, out_means = refs[13:17]
    e, g, x, y, d, kf, wf, kx, ky, ox, oy, edges = refs[17:29]
    rows, cols = fine[0].shape
    own = cols // LANES
    tiles = own + 1
    pairs_only = block_size == 2
    n = rows // 8 + (HALO // 8) * (1 if pairs_only else 2)
    gx, grid, first, last = place_of(block_size)
    gx_is_even = lax.rem(gx, 2) == 0
    gy_is_even = lax.rem(lax.axis_index("gy"), 2) == 0
    lane = iota((8, LANES), 1)
    sub = iota((8, LANES), 0)

    def unpack(from_even, from_odd, f):
        from_east = jnp.where(gy_is_even, from_even, from_odd)
        from_west = jnp.where(gy_is_even, from_odd, from_even)
        east = roll_to(from_east, 16 * f, 0)
        west = roll_to(from_west, 16 * f, LANES - 16)
        return jnp.where(lane < 16, east, jnp.where(lane >= LANES - 16, west, 0.0))

    dest = (e, x, y, d, kf, wf)
    for r in range(rows // 8):
        src, here = pl.ds(8 * r, 8), pl.ds(8 + 8 * r, 8)
        for t in range(own):
            for f, value in enumerate(fine_fields(fine, src, pl.ds(t * LANES, LANES), table)):
                dest[f][t, here, :] = value
        for f in range(6):
            dest[f][own, here, :] = unpack(gy_even[src, :], gy_odd[src, :], f)

    def halo_rows(messages, base):
        for half in range(HALO // 8):
            here = pl.ds(8 + base + 8 * half, 8)

            def take(block):
                picked = [m[pl.ds(block * HALO + 8 * half, 8), :] for m in messages]
                return picked[0] if len(picked) == 1 else jnp.where(gx_is_even, picked[0], picked[1])

            for f in range(6):
                for t in range(own):
                    dest[f][t, here, :] = take(f * own + t)
                dest[f][own, here, :] = unpack(take(6 * own), take(6 * own + 1), f)

    if pairs_only:
        halo_rows([gx_even], rows)
    else:
        halo_rows([gx_even, gx_odd], rows)
        halo_rows([gx_odd, gx_even], rows + HALO)

    ocean_rows = ocean_mx.shape[0]
    own_offset = offsets[grid]
    at = own_offset - 1
    mx_own = ocean_mx[...] * SB
    from_east = jnp.where(gy_is_even, gy_even[0:ocean_rows, :], gy_odd[0:ocean_rows, :])
    from_west = jnp.where(gy_is_even, gy_odd[0:ocean_rows, :], gy_even[0:ocean_rows, :])
    lanes = iota((ocean_rows, LANES), 1)
    mx_halo = jnp.where(
        lanes < 4, roll_to(from_east, OLANE + 4, 0), roll_to(from_west, OLANE + 4, LANES - 4)
    )
    picks = iota((8, ocean_rows), 1) == jnp.where(iota((8, ocean_rows), 0) == 0, at, ocean_rows - 1)
    picks = picks.astype(F32)
    source = jnp.concatenate([dot(picks, mx_own), dot(picks, mx_halo)], 1)
    fine_lane = iota((2 * LANES, tiles * LANES), 1)
    ocean_lane = iota((2 * LANES, tiles * LANES), 0)
    width = own * LANES
    wanted = jnp.where(
        fine_lane < width + 64,
        lax.div(fine_lane, R),
        2 * LANES - 1 - lax.div(tiles * LANES - 1 - fine_lane, R),
    )
    spread = dot(source, (ocean_lane == wanted).astype(F32))
    for t in range(tiles):
        cut = spread[:, t * LANES : (t + 1) * LANES]
        wet_first = wf[t, pl.ds(8, 8), :]
        wet_last = wf[t, pl.ds(8 + rows - 8, 8), :]
        edges[0, t, :, :] = jnp.broadcast_to(cut[0:1, :] * wet_first[0:1, :], (8, LANES))
        edges[1, t, :, :] = jnp.broadcast_to(cut[1:2, :] * wet_last[7:8, :], (8, LANES))

    prepare_faces(tiles, n, kf, wf, kx, ky, ox, oy)

    west_mask = (sub == 7) & first
    east_mask = (sub == 7) & last

    def fix(r, t, fx):
        if r == rows // 8 - 1:
            fx = jnp.where(east_mask, edges[1, t, :, :], fx)
        if r == n - 1:
            fx = jnp.where(west_mask, edges[0, t, :, :], fx)
        return fx

    for t in range(tiles):
        start = jnp.where(west_mask, edges[0, t, :, :], x[t, pl.ds(8 * n, 8), :])
        x[t, pl.ds(0, 8), :] = start

    def step(_, carry):
        level_pass(tiles, n, e, g, x, y, d)
        flux_pass(tiles, n, e, g, x, y, kx, ky, ox, oy, fix)
        return carry

    lax.fori_loop(0, FSTEPS, step, 0)

    for r in range(rows // 8):
        to, here = pl.ds(8 * r, 8), pl.ds(8 + 8 * r, 8)
        for t in range(own):
            at_cols = pl.ds(t * LANES, LANES)
            out_eta[to, at_cols] = e[t, here, :] * (1.0 / SA)
            out_x[to, at_cols] = x[t, here, :] * (1.0 / SB)
            out_y[to, at_cols] = y[t, here, :] * (1.0 / SB)

    coarse_row = lax.rem(lax.div(iota((ocean_rows, rows), 1), R) + own_offset, ocean_rows)
    gather_rows = (coarse_row == iota((ocean_rows, rows), 0)).astype(F32)
    gather_cols = (lax.div(iota((cols, LANES), 0), R) == iota((cols, LANES), 1)).astype(F32)
    out_means[...] = dot(dot(gather_rows, out_eta[...]), gather_cols) * (1.0 / (R * R))


def ocean_kernel(pairs_only, *refs):
    table, ocean = refs[0], refs[1:6]
    gy_even, gy_odd, gx_even, gx_odd = refs[6:10]
    out_eta, out_x, out_y = refs[10:13]
    e, g, x, y, d, kf, kx, ky, ox, oy = refs[13:23]
    rows, cols = ocean[0].shape
    tiles = 2
    n = rows // 8 + 1
    gx, gy = lax.axis_index("gx"), lax.axis_index("gy")
    gx_is_even = lax.rem(gx, 2) == 0
    gy_is_even = lax.rem(gy, 2) == 0
    lane = iota((8, LANES), 1)
    sub = iota((8, LANES), 0)

    def unpack(from_even, from_odd, j):
        from_east = jnp.where(gy_is_even, from_even, from_odd)
        from_west = jnp.where(gy_is_even, from_odd, from_even)
        east = roll_to(from_east, OLANE + 4 * j, 0)
        west = roll_to(from_west, OLANE + 4 * j, LANES - 4)
        return jnp.where(lane < 4, east, jnp.where(lane >= LANES - 4, west, 0.0))

    dest = (e, x, y, d, kf)
    for r in range(rows // 8):
        src, here = pl.ds(8 * r, 8), pl.ds(8 + 8 * r, 8)
        for j, value in enumerate(ocean_fields(ocean, src, pl.ds(0, LANES), table)):
            dest[j][0, here, :] = value
            dest[j][1, here, :] = unpack(gy_even[src, :], gy_odd[src, :], j)

    def take(block):
        start_even = gx_even.shape[0] - 56
        start_odd = gx_odd.shape[0] - 56
        first = gx_even[pl.ds(start_even + 8 * block, 8), :]
        second = gx_odd[pl.ds(start_odd + 8 * block, 8), :]
        after = jnp.where(gx_is_even, first, second)
        before = jnp.where(gx_is_even, second, first)
        return jnp.where(sub < 4, after, before)

    here = pl.ds(8 + rows, 8)
    for j in range(5):
        dest[j][0, here, :] = take(j)
        dest[j][1, here, :] = unpack(take(5), take(6), j)

    prepare_faces(tiles, n, kf, None, kx, ky, None, None)
    rows_total, cols_total = rows * lax.axis_size("gx"), cols * lax.axis_size("gy")
    for r in range(n):
        here = pl.ds(8 + 8 * r, 8)
        row = sub + 8 * r
        row = jnp.where(row >= rows + 4, row - (rows + 8), row) + gx * rows
        for t in range(tiles):
            col = lane if t == 0 else jnp.where(lane < 64, lane + LANES, lane - LANES)
            col = col + gy * cols
            ox[t, here, :] = jnp.where((row >= 0) & (row < rows_total - 1), 1.0, CLOSED)
            oy[t, here, :] = jnp.where((col >= 0) & (col < cols_total - 1), 1.0, CLOSED)
    for t in range(tiles):
        x[t, pl.ds(0, 8), :] = x[t, pl.ds(8 * n, 8), :]

    def step(_, carry):
        level_pass(tiles, n, e, g, x, y, d)
        flux_pass(tiles, n, e, g, x, y, kx, ky, ox, oy, lambda r, t, fx: fx)
        return carry

    lax.fori_loop(0, ITERS, step, 0)
    for r in range(rows // 8):
        to, here = pl.ds(8 * r, 8), pl.ds(8 + 8 * r, 8)
        out_eta[to, :] = e[0, here, :] * (1.0 / SA)
        out_x[to, :] = x[0, here, :] * (1.0 / SB)
        out_y[to, :] = y[0, here, :] * (1.0 / SB)


def paste_kernel(block_size, *refs):
    offsets, eta, rolled, arrived, out = refs
    gx, grid, _, _ = place_of(block_size)
    own_offset = offsets[grid]
    left_offset = jnp.where(gx >= 1, offsets[lax.div(jnp.maximum(gx - 1, 0), block_size)], 0)
    row = iota(eta.shape, 0)
    out[...] = jnp.where(
        row >= own_offset, rolled[...], jnp.where(row < left_offset, arrived[...], eta[...])
    )


def shape(*dims):
    return jax.ShapeDtypeStruct(dims, F32)


def params():
    return pltpu.CompilerParams(vmem_limit_bytes=48 * 1024 * 1024)


def cost(ops, size):
    return pl.CostEstimate(flops=ops, bytes_accessed=size, transcendentals=0)


def shards(
    ocean_eta,
    ocean_mx,
    ocean_ny,
    ocean_depth,
    ocean_class,
    manning,
    fine_eta,
    fine_qx,
    fine_qy,
    fine_depth,
    fine_wet,
    fine_class,
    fine_offset,
):
    ocean_rows, ocean_cols = ocean_eta.shape
    rows, cols = fine_eta.shape
    own = cols // LANES
    gx_count = lax.axis_size("gx")
    block_size = min(16, gx_count // 2)
    pairs_only = block_size == 2
    fine = (fine_eta, fine_qx, fine_qy, fine_depth, fine_wet, fine_class)
    ocean = (ocean_eta, ocean_mx, ocean_ny, ocean_depth, ocean_class)

    gy_even, gy_odd = pl.pallas_call(
        functools.partial(pack_columns_kernel, cols),
        out_shape=(shape(rows, LANES), shape(rows, LANES)),
        in_specs=[SMEM] + [VMEM] * 11,
        out_specs=(VMEM, VMEM),
        compiler_params=params(),
        name="pack_columns",
    )(manning, *fine, *ocean)
    gy_even = swap_even(gy_even, "gy")
    gy_odd = swap_odd(gy_odd, "gy")

    fine_rows = (6 * own + 2) * HALO
    gx_even, gx_odd = pl.pallas_call(
        functools.partial(pack_rows_kernel, pairs_only),
        out_shape=(shape(fine_rows + 56, LANES), shape(56 + (0 if pairs_only else fine_rows), LANES)),
        in_specs=[SMEM] + [VMEM] * 13,
        out_specs=(VMEM, VMEM),
        compiler_params=params(),
        name="pack_rows",
    )(manning, *fine, *ocean, gy_even, gy_odd)
    gx_even = swap_even(gx_even, "gx")
    gx_odd = swap_odd(gx_odd, "gx")

    n = rows // 8 + (HALO // 8) * (1 if pairs_only else 2)
    tiles = own + 1
    scratch = [pltpu.VMEM((tiles, 8 * n + 16, LANES), F32)] * 11 + [pltpu.VMEM((2, tiles, 8, LANES), F32)]
    feta, fqx, fqy, rolled = pl.pallas_call(
        functools.partial(fine_kernel, block_size),
        out_shape=(shape(rows, cols),) * 3 + (shape(ocean_rows, ocean_cols),),
        in_specs=[SMEM, SMEM] + [VMEM] * 11,
        out_specs=(VMEM,) * 4,
        scratch_shapes=scratch,
        compiler_params=params(),
        name="coastal",
    )(manning, fine_offset, *fine, ocean_mx, gy_even, gy_odd, gx_even, gx_odd)
    arrived = lax.ppermute(rolled, "gx", [(i, i + 1) for i in range(gx_count - 1)])

    n = ocean_rows // 8 + 1
    eta, mx, ny = pl.pallas_call(
        functools.partial(ocean_kernel, pairs_only),
        out_shape=(shape(ocean_rows, ocean_cols),) * 3,
        in_specs=[SMEM] + [VMEM] * 9,
        out_specs=(VMEM,) * 3,
        scratch_shapes=[pltpu.VMEM((2, 8 * n + 16, LANES), F32)] * 10,
        compiler_params=params(),
        name="ocean",
    )(manning, *ocean, gy_even, gy_odd, gx_even, gx_odd)

    eta = pl.pallas_call(
        functools.partial(paste_kernel, block_size),
        out_shape=shape(ocean_rows, ocean_cols),
        in_specs=[SMEM] + [VMEM] * 3,
        out_specs=VMEM,
        compiler_params=params(),
        name="paste",
    )(fine_offset, eta, rolled, arrived)
    return (eta, mx, ny, feta, fqx, fqy)


def solution(mesh):
    tile = P(("scen", "gx"), "gy")
    in_specs = (tile,) * 5 + (P(),) + (tile,) * 6 + (P("scen"),)
    return jax.shard_map(shards, mesh=mesh, in_specs=in_specs, out_specs=(tile,) * 6, check_vma=False)
```

```python
import functools

import jax
import jax.numpy as jnp
from jax import lax
from jax.experimental import pallas as pl
from jax.experimental.pallas import tpu as pltpu
from jax.sharding import PartitionSpec as P

R = 3
ITERS = 4
FSTEPS = R * ITERS
COURANT = 0.45
FLOOR = 0.25
SA = COURANT**2 / 2
SB = COURANT**3 / 2
POWER = -7.0 / 3.0
TFLOOR = 2 * SA * FLOOR
KSCALE = 0.5 * COURANT * (2 * SA) ** (7.0 / 3.0) / SB
CLOSED = 3.0e38
LANES = 128
HALO = 16
OLANE = 6 * 16
REACH = FSTEPS
VMEM = pl.BlockSpec(memory_space=pltpu.VMEM)
SMEM = pl.BlockSpec(memory_space=pltpu.SMEM)
ANY = pl.BlockSpec(memory_space=pltpu.HBM)
F32 = jnp.float32


def swap_even(value, axis):
    count = lax.axis_size(axis)
    return lax.ppermute(value, axis, [(i, i ^ 1) for i in range(count) if i ^ 1 < count])


def swap_odd(value, axis):
    count = lax.axis_size(axis)
    pairs = [(i, ((i + 1) ^ 1) - 1) for i in range(1, count)]
    return lax.ppermute(value, axis, [(a, b) for a, b in pairs if b < count])


def friction(classes, table):
    result = jnp.full(classes.shape, table[0], F32)
    for level_id in range(1, table.shape[0]):
        result = jnp.where(classes == level_id, table[level_id], result)
    return result


def field_of(refs, f, rows, cols, table):
    value = refs[f][rows, cols]
    if f < 4:
        return value * (SA, SB, SB, SA)[f]
    return friction(value, table) if f == 4 else value.astype(F32)


def fine_fields(refs, rows, cols, table):
    eta, qx, qy, depth, wet, classes = refs
    return tuple(field_of((eta, qx, qy, depth, classes, wet), f, rows, cols, table) for f in range(6))


def ocean_field(refs, j, rows, cols, table):
    value = refs[j][rows, cols]
    return value * (SA, SB, SB, SA)[j] if j < 4 else friction(value, table)


def ocean_fields(refs, rows, cols, table):
    return tuple(ocean_field(refs, j, rows, cols, table) for j in range(5))


def roll_to(value, start, target):
    return pltpu.roll(value, (target - start) % LANES, 1)


def copy_in(pairs, sems):
    copies = [pltpu.make_async_copy(src, dst, sems.at[i]) for i, (src, dst) in enumerate(pairs)]
    for copy in copies:
        copy.start()
    for copy in copies:
        copy.wait()


def pack_rows_kernel(pairs_only, *refs):
    table, fine, ocean = refs[0], refs[1:7], refs[7:12]
    outs = refs[12:14]
    held, held_int, ocean_in, ocean_class, sems = refs[14:]
    rows, cols = fine[0].shape
    tiles = cols // LANES
    ocean_rows = ocean[0].shape[0]
    is_even = lax.rem(lax.axis_index("gx"), 2) == 0
    pairs = []
    for side in range(1 if pairs_only else 2):
        last = is_even if side == 0 else jnp.logical_not(is_even)
        at = pl.multiple_of(jnp.where(last, rows - HALO, 0), 8)
        for f in range(6):
            target = held.at[f, side] if f < 4 else held_int.at[f - 4, side]
            pairs.append((fine[f].at[pl.ds(at, HALO), :], target))
    for j in range(5):
        pairs.append((ocean[j], ocean_in.at[j] if j < 4 else ocean_class))
    copy_in(pairs, sems)

    for side, out in enumerate(outs):
        last = is_even if side == 0 else jnp.logical_not(is_even)
        base = out.shape[0] - 5 * ITERS
        if base > 0:
            sources = [held.at[f, side] for f in range(4)] + [held_int.at[f, side] for f in range(2)]
            for t in range(tiles):
                at_cols = pl.ds(t * LANES, LANES)
                low = fine_fields(sources, pl.ds(HALO - REACH, REACH), at_cols, table)
                top = fine_fields(sources, pl.ds(0, REACH), at_cols, table)
                for f in range(6):
                    out[pl.ds((f * tiles + t) * REACH, REACH), :] = jnp.where(last, low[f], top[f])
        sources = [ocean_in.at[j] for j in range(4)] + [ocean_class]
        low = ocean_fields(sources, pl.ds(ocean_rows - ITERS, ITERS), pl.ds(0, LANES), table)
        top = ocean_fields(sources, pl.ds(0, ITERS), pl.ds(0, LANES), table)
        for j in range(5):
            out[pl.ds(base + j * ITERS, ITERS), :] = jnp.where(last, low[j], top[j])


def halo_blocks(pairs_only, messages, block, gx_is_even):
    rows = [message[pl.ds(block * REACH, REACH), :] for message in messages[: 1 if pairs_only else 2]]
    gap = jnp.zeros((HALO - REACH, LANES), F32)
    if pairs_only:
        return [jnp.where(gx_is_even, jnp.concatenate([rows[0], gap], 0), jnp.concatenate([gap, rows[0]], 0))]
    after = jnp.where(gx_is_even, rows[0], rows[1])
    before = jnp.where(gx_is_even, rows[1], rows[0])
    return [jnp.concatenate([after, gap], 0), jnp.concatenate([gap, before], 0)]


def ocean_halo(messages, j, gx_is_even):
    even, odd = (m[pl.ds(m.shape[0] - (5 - j) * ITERS, ITERS), :] for m in messages)
    return jnp.where(gx_is_even, jnp.concatenate([even, odd], 0), jnp.concatenate([odd, even], 0))


def packed_columns(parts):
    lane = iota((8, LANES), 1)
    west = jnp.zeros((8, LANES), F32)
    east = jnp.zeros((8, LANES), F32)
    for at, wide, from_west, from_east in parts:
        inside = (lane >= at) & (lane < at + wide)
        west = jnp.where(inside, roll_to(from_west, 0, at), west)
        east = jnp.where(inside, roll_to(from_east, LANES - wide, at), east)
    is_even = lax.rem(lax.axis_index("gy"), 2) == 0
    return jnp.where(is_even, east, west), jnp.where(is_even, west, east)


def columns_parts(first, last, ocean_values):
    parts = [(16 * f, 16, first[f], last[f]) for f in range(6)]
    return parts + [(OLANE + ITERS * j, ITERS, v, v) for j, v in enumerate(ocean_values)]


def strip_lanes(first, last):
    lane = iota((8, LANES), 1)
    moved = jnp.where(lane < 64, roll_to(last, LANES - 32, 32), 0.0)
    return jnp.where(lane < 32, first, moved)


def prepare_kernel(*refs):
    table, fine, ocean = refs[0], refs[1:7], refs[7:12]
    even_out, odd_out, strip = refs[12:]
    rows, cols = fine[0].shape
    ocean_rows = ocean[0].shape[0]
    for r in range(rows // 8):
        row = pl.ds(8 * r, 8)
        first = fine_fields(fine, row, pl.ds(0, LANES), table)
        last = fine_fields(fine, row, pl.ds(cols - LANES, LANES), table)
        values = ocean_fields(ocean, row, pl.ds(0, LANES), table) if 8 * r < ocean_rows else ()
        even_out[row, :], odd_out[row, :] = packed_columns(columns_parts(first, last, values))
        for f in range(6):
            strip[f, row, :] = strip_lanes(first[f], last[f])


def pack_columns_kernel(pairs_only, tiles, ocean_rows, *refs):
    own, messages, outs = refs[:2], refs[2:4], refs[4:6]
    rows = own[0].shape[0]
    gx_is_even = lax.rem(lax.axis_index("gx"), 2) == 0
    extra = pl.ds(ocean_rows, 8)
    values = [ocean_halo(messages, j, gx_is_even) for j in range(5)]
    parts = [(OLANE + ITERS * j, ITERS, v, v) for j, v in enumerate(values)]
    ocean_lanes = iota((8, LANES), 1) >= OLANE
    for out, mine, value in zip(outs, own, packed_columns(parts)):
        out[0:rows, :] = mine[...]
        out[extra, :] = jnp.where(ocean_lanes, value, mine[extra, :])
    halos = [
        [halo_blocks(pairs_only, messages, f * tiles + t, gx_is_even) for t in (0, tiles - 1)] for f in range(6)
    ]
    for r in range(rows // 8, outs[0].shape[0] // 8):
        side, half = divmod(r - rows // 8, HALO // 8)
        first, last = (
            [halos[f][end][side][8 * half : 8 * half + 8] for f in range(6)] for end in range(2)
        )
        for out, value in zip(outs, packed_columns(columns_parts(first, last, ()))):
            out[pl.ds(8 * r, 8), :] = value


def lane_next(values, ring=True):
    lane = lax.broadcasted_iota(jnp.int32, values[0].shape, 1)
    rolled = [pltpu.roll(v, LANES - 1, 1) for v in values]
    count = len(values)
    if count == 1:
        return rolled
    inner = [jnp.where(lane == LANES - 1, rolled[t + 1], rolled[t]) for t in range(count - 1)]
    end = jnp.where(lane == LANES - 1, rolled[0], rolled[-1]) if ring else rolled[-1]
    return inner + [end]


def lane_prev(values, ring=True):
    lane = lax.broadcasted_iota(jnp.int32, values[0].shape, 1)
    rolled = [pltpu.roll(v, 1, 1) for v in values]
    count = len(values)
    if count == 1:
        return rolled
    start = jnp.where(lane == 0, rolled[-1] if ring else 0.0, rolled[0])
    return [start] + [jnp.where(lane == 0, rolled[t - 1], rolled[t]) for t in range(1, count)]


def new_flux(flux, eta, eta_next, wet, wet_next, opened, drag):
    total = wet + wet_next
    power = jnp.exp2(POWER * jnp.log2(jnp.maximum(total, TFLOOR)))
    denom = opened + (drag * jnp.abs(flux)) * power
    return (flux - total * (eta_next - eta)) / denom


def prepare_faces(tiles, n, kf, wf, kx, ky, ox, oy, ring=True):
    for t in range(tiles):
        wrap = pl.ds(8 + 8 * n, 8)
        kf[t, wrap, :] = kf[t, pl.ds(8, 8), :]
        if wf is not None:
            wf[t, wrap, :] = wf[t, pl.ds(8, 8), :]
    for r in range(n):
        here, after = pl.ds(8 + 8 * r, 8), pl.ds(9 + 8 * r, 8)
        k = [kf[t, here, :] for t in range(tiles)]
        k_next = lane_next(k)
        if wf is not None:
            w = [wf[t, here, :] for t in range(tiles)]
            w_next = lane_next(w)
        for t in range(tiles):
            kx[t, here, :] = KSCALE * (k[t] + kf[t, after, :])
            ky[t, here, :] = KSCALE * (k[t] + k_next[t])
            if wf is not None:
                ox[t, here, :] = jnp.where(w[t] * wf[t, after, :] > 0.5, 1.0, CLOSED)
                open_y = w[t] * w_next[t] > 0.5
                if not ring and t == tiles - 1:
                    open_y = open_y & (iota((8, LANES), 1) < LANES - 1)
                oy[t, here, :] = jnp.where(open_y, 1.0, CLOSED)


def level_pass(tiles, n, e, g, x, y, d, ring=True):
    for r in range(n):
        here, before = pl.ds(8 + 8 * r, 8), pl.ds(7 + 8 * r, 8)
        south = [y[t, here, :] for t in range(tiles)]
        south_prev = lane_prev(south, ring)
        for t in range(tiles):
            flow = (x[t, here, :] - x[t, before, :]) + (south[t] - south_prev[t])
            eta = e[t, here, :] - flow
            wet = jnp.maximum(d[t, here, :] + eta, 0.0)
            e[t, here, :] = eta
            g[t, here, :] = wet
            if r == 0:
                e[t, pl.ds(8 + 8 * n, 8), :] = eta
                g[t, pl.ds(8 + 8 * n, 8), :] = wet


def flux_pass(tiles, n, e, g, x, y, kx, ky, ox, oy, fix, ring=True):
    for r in range(n):
        here, after = pl.ds(8 + 8 * r, 8), pl.ds(9 + 8 * r, 8)
        eta = [e[t, here, :] for t in range(tiles)]
        wet = [g[t, here, :] for t in range(tiles)]
        eta_next, wet_next = lane_next(eta, ring), lane_next(wet, ring)
        for t in range(tiles):
            fx = new_flux(
                x[t, here, :], eta[t], e[t, after, :], wet[t], g[t, after, :], ox[t, here, :], kx[t, here, :]
            )
            fx = fix(r, t, fx)
            x[t, here, :] = fx
            if r == n - 1:
                x[t, pl.ds(0, 8), :] = fx
            y[t, here, :] = new_flux(
                y[t, here, :], eta[t], eta_next[t], wet[t], wet_next[t], oy[t, here, :], ky[t, here, :]
            )


def dot(a, b):
    return lax.dot_general(
        a, b, (((1,), (0,)), ((), ())), precision=lax.Precision.HIGHEST, preferred_element_type=F32
    )


def iota(shape, dim):
    return lax.broadcasted_iota(jnp.int32, shape, dim)


def place_of(block_size):
    gx = lax.axis_index("gx")
    slot = lax.rem(gx, block_size)
    return gx, lax.div(gx, block_size), slot == 0, slot == block_size - 1


def grid_edges(mx_tiles, own_offset, ocean_rows, spread_to, wf, rows, edges):
    picks = iota((8, ocean_rows), 1) == jnp.where(iota((8, ocean_rows), 0) == 0, own_offset - 1, ocean_rows - 1)
    picks = picks.astype(F32)
    source = jnp.concatenate([dot(picks, tile) for tile in mx_tiles], 1)
    spread = dot(source, spread_to.astype(F32))
    for t in range(edges.shape[1]):
        cut = spread[:, t * LANES : (t + 1) * LANES]
        wet_first = wf[t, pl.ds(8, 8), :]
        wet_last = wf[t, pl.ds(rows, 8), :]
        edges[0, t, :, :] = jnp.broadcast_to(cut[0:1, :] * wet_first[0:1, :], (8, LANES))
        edges[1, t, :, :] = jnp.broadcast_to(cut[1:2, :] * wet_last[7:8, :], (8, LANES))


def run_coastal(tiles, n, rows, first, last, state, edges, ring):
    e, g, x, y, d, kx, ky, ox, oy = state
    sub = iota((8, LANES), 0)
    west_mask = (sub == 7) & first
    east_mask = (sub == 7) & last

    def fix(r, t, fx):
        if r == rows // 8 - 1:
            fx = jnp.where(east_mask, edges[1, t, :, :], fx)
        if r == n - 1:
            fx = jnp.where(west_mask, edges[0, t, :, :], fx)
        return fx

    for t in range(tiles):
        x[t, pl.ds(0, 8), :] = jnp.where(west_mask, edges[0, t, :, :], x[t, pl.ds(8 * n, 8), :])

    def step(_, carry):
        level_pass(tiles, n, e, g, x, y, d, ring)
        flux_pass(tiles, n, e, g, x, y, kx, ky, ox, oy, fix, ring)
        return carry

    lax.fori_loop(0, FSTEPS, step, 0)


def interior_kernel(block_size, *refs):
    table, offsets, fine, ocean_mx = refs[0], refs[1], refs[2:8], refs[8]
    pairs_only = block_size == 2
    count = 1 if pairs_only else 2
    messages = refs[9:11]
    outs, out_means = refs[11:14], refs[14]
    e, g, x, y, d, kf, wf, kx, ky, ox, oy, edges = refs[15:]
    rows, cols = fine[0].shape
    tiles = cols // LANES
    n = rows // 8 + (HALO // 8) * count
    gx, grid, first, last = place_of(block_size)
    gx_is_even = lax.rem(gx, 2) == 0
    dest = (e, x, y, d, kf, wf)
    for r in range(rows // 8):
        src, here = pl.ds(8 * r, 8), pl.ds(8 + 8 * r, 8)
        for t in range(tiles):
            for f, value in enumerate(fine_fields(fine, src, pl.ds(t * LANES, LANES), table)):
                dest[f][t, here, :] = value
    for f in range(6):
        for t in range(tiles):
            for side, block in enumerate(halo_blocks(pairs_only, messages, f * tiles + t, gx_is_even)):
                dest[f][t, pl.ds(8 + rows + HALO * side, HALO), :] = block

    ocean_rows = ocean_mx.shape[0]
    spread_to = iota((LANES, cols), 0) == lax.div(iota((LANES, cols), 1), R)
    grid_edges([ocean_mx[...] * SB], offsets[grid], ocean_rows, spread_to, wf, rows, edges)
    prepare_faces(tiles, n, kf, wf, kx, ky, ox, oy, False)
    run_coastal(tiles, n, rows, first, last, (e, g, x, y, d, kx, ky, ox, oy), edges, False)
    for r in range(rows // 8):
        to, here = pl.ds(8 * r, 8), pl.ds(8 + 8 * r, 8)
        for t in range(tiles):
            at_cols = pl.ds(t * LANES, LANES)
            outs[0][to, at_cols] = e[t, here, :] * (1.0 / SA)
            outs[1][to, at_cols] = x[t, here, :] * (1.0 / SB)
            outs[2][to, at_cols] = y[t, here, :] * (1.0 / SB)
    gather_cols = (lax.div(iota((cols, LANES), 0), R) == iota((cols, LANES), 1)).astype(F32)
    out_means[...] = coarse_means(outs[0][...], gather_cols, offsets[grid], ocean_rows)


def coarse_means(eta, gather_cols, own_offset, ocean_rows):
    shape = (ocean_rows, eta.shape[0])
    coarse_row = lax.rem(lax.div(iota(shape, 1), R) + own_offset, ocean_rows)
    gather_rows = (coarse_row == iota(shape, 0)).astype(F32)
    return dot(dot(gather_rows, eta), gather_cols) * (1.0 / (R * R))


def border_kernel(block_size, cols, *refs):
    offsets, strip, ocean_mx, messages = refs[0], refs[1], refs[2], refs[3:5]
    gy_even, gy_odd, inner_means = refs[5:8]
    outs, out_means = refs[8:11], refs[11]
    e, g, x, y, d, kf, wf, kx, ky, ox, oy, edges = refs[12:]
    pairs_only = block_size == 2
    rows = strip.shape[1]
    own = cols // LANES
    n = rows // 8 + (HALO // 8) * (1 if pairs_only else 2)
    gx, grid, first, last = place_of(block_size)
    gx_is_even = lax.rem(gx, 2) == 0
    gy_is_even = lax.rem(lax.axis_index("gy"), 2) == 0
    lane = iota((8, LANES), 1)
    dest = (e, x, y, d, kf, wf)
    halos = [
        [halo_blocks(pairs_only, messages, f * own + t, gx_is_even) for t in (0, own - 1)] for f in range(6)
    ]
    for r in range(n):
        src, here = pl.ds(8 * r, 8), pl.ds(8 + 8 * r, 8)
        if 8 * r < rows:
            mine = [strip[f, src, :] for f in range(6)]
        else:
            side, half = divmod(r - rows // 8, HALO // 8)
            cut = slice(8 * half, 8 * half + 8)
            mine = [strip_lanes(halos[f][0][side][cut], halos[f][1][side][cut]) for f in range(6)]
        from_even, from_odd = gy_even[src, :], gy_odd[src, :]
        from_east = jnp.where(gy_is_even, from_even, from_odd)
        from_west = jnp.where(gy_is_even, from_odd, from_even)
        for f in range(6):
            east = roll_to(from_east, 16 * f, 64)
            west = roll_to(from_west, 16 * f, LANES - 16)
            value = jnp.where((lane >= 64) & (lane < 80), east, mine[f])
            dest[f][0, here, :] = jnp.where(lane < LANES - 16, value, west)

    ocean_rows = ocean_mx.shape[0]
    from_even, from_odd = gy_even[0:ocean_rows, :], gy_odd[0:ocean_rows, :]
    from_east = jnp.where(gy_is_even, from_even, from_odd)
    from_west = jnp.where(gy_is_even, from_odd, from_even)
    lanes = iota((ocean_rows, LANES), 1)
    mx_halo = jnp.where(
        lanes < ITERS,
        roll_to(from_east, OLANE + ITERS, 0),
        roll_to(from_west, OLANE + ITERS, LANES - ITERS),
    )
    to = iota((2 * LANES, LANES), 1)
    wanted = jnp.where(to < 32, lax.div(to, R), lax.div(to + (cols - 64), R))
    wanted = jnp.where(to < 64, wanted, jnp.where(to < 80, LANES + lax.div(to - 64, R), 0))
    wanted = jnp.where(to < LANES - 16, wanted, 2 * LANES - 1 - lax.div(LANES - 1 - to, R))
    spread_to = iota((2 * LANES, LANES), 0) == wanted
    grid_edges([ocean_mx[...] * SB, mx_halo], offsets[grid], ocean_rows, spread_to, wf, rows, edges)
    prepare_faces(1, n, kf, wf, kx, ky, ox, oy)
    run_coastal(1, n, rows, first, last, (e, g, x, y, d, kx, ky, ox, oy), edges, True)

    for i, (held, scale) in enumerate(((e, 1.0 / SA), (x, 1.0 / SB), (y, 1.0 / SB))):
        outs[i][...] = held[0, 8 : 8 + rows, :] * scale
    source, target = iota((LANES, LANES), 0), iota((LANES, LANES), 1)
    column = jnp.where(source < 32, source, source + (cols - 64))
    inside = (source < FSTEPS) | ((source >= 64 - FSTEPS) & (source < 64))
    gather = ((lax.div(column, R) == target) & inside).astype(F32)
    means = coarse_means(outs[0][...], gather, offsets[grid], ocean_rows)
    col = iota((ocean_rows, LANES), 1)
    out_means[...] = jnp.where((col < ITERS) | (col >= LANES - ITERS), means, inner_means[...])


def finish_coastal(inner, strips, final, outs, sems):
    rows, cols = final.shape[1:]
    own = cols // LANES
    lane = iota((8, LANES), 1)
    copies = [pltpu.make_async_copy(final.at[i], outs[i], sems.at[i]) for i in range(3)]
    for i in range(3):
        for r in range(rows // 8):
            to = pl.ds(8 * r, 8)
            value = strips[i][to, :]
            for t in range(own):
                at_cols = pl.ds(t * LANES, LANES)
                kept = inner[i][to, at_cols]
                if t == 0:
                    kept = jnp.where(lane < FSTEPS, value, kept)
                if t == own - 1:
                    kept = jnp.where(lane >= LANES - FSTEPS, roll_to(value, 32, LANES - 32), kept)
                final[i, to, at_cols] = kept
        copies[i].start()
    return copies


def finish_kernel(*refs):
    table, ocean = refs[0], refs[1:6]
    gy_even, gy_odd, gx_even, gx_odd = refs[6:10]
    inner, strips = refs[10:13], refs[13:16]
    fine_outs, (out_eta, out_x, out_y) = refs[16:19], refs[19:22]
    final, sems = refs[22:24]
    e, g, x, y, d, kf, kx, ky, ox, oy = refs[24:]
    copies = finish_coastal(inner, strips, final, fine_outs, sems)
    rows, cols = ocean[0].shape
    tiles = 2
    n = rows // 8 + 1
    gx, gy = lax.axis_index("gx"), lax.axis_index("gy")
    gx_is_even = lax.rem(gx, 2) == 0
    gy_is_even = lax.rem(gy, 2) == 0
    lane = iota((8, LANES), 1)
    sub = iota((8, LANES), 0)

    def unpack(from_even, from_odd, j):
        from_east = jnp.where(gy_is_even, from_even, from_odd)
        from_west = jnp.where(gy_is_even, from_odd, from_even)
        east = roll_to(from_east, OLANE + ITERS * j, 0)
        west = roll_to(from_west, OLANE + ITERS * j, LANES - 4)
        return jnp.where(lane < 4, east, jnp.where(lane >= LANES - 4, west, 0.0))

    dest = (e, x, y, d, kf)
    for r in range(rows // 8):
        src, here = pl.ds(8 * r, 8), pl.ds(8 + 8 * r, 8)
        for j, value in enumerate(ocean_fields(ocean, src, pl.ds(0, LANES), table)):
            dest[j][0, here, :] = value
            dest[j][1, here, :] = unpack(gy_even[src, :], gy_odd[src, :], j)

    here, halo = pl.ds(8 + rows, 8), pl.ds(rows, 8)
    for j in range(5):
        dest[j][0, here, :] = ocean_halo((gx_even, gx_odd), j, gx_is_even)
        dest[j][1, here, :] = unpack(gy_even[halo, :], gy_odd[halo, :], j)

    prepare_faces(tiles, n, kf, None, kx, ky, None, None)
    rows_total, cols_total = rows * lax.axis_size("gx"), cols * lax.axis_size("gy")
    for r in range(n):
        here = pl.ds(8 + 8 * r, 8)
        row = sub + 8 * r
        row = jnp.where(row >= rows + 4, row - (rows + 8), row) + gx * rows
        for t in range(tiles):
            col = lane if t == 0 else jnp.where(lane < 64, lane + LANES, lane - LANES)
            col = col + gy * cols
            ox[t, here, :] = jnp.where((row >= 0) & (row < rows_total - 1), 1.0, CLOSED)
            oy[t, here, :] = jnp.where((col >= 0) & (col < cols_total - 1), 1.0, CLOSED)
    for t in range(tiles):
        x[t, pl.ds(0, 8), :] = x[t, pl.ds(8 * n, 8), :]

    def step(_, carry):
        level_pass(tiles, n, e, g, x, y, d)
        flux_pass(tiles, n, e, g, x, y, kx, ky, ox, oy, lambda r, t, fx: fx)
        return carry

    lax.fori_loop(0, ITERS, step, 0)
    for r in range(rows // 8):
        to, here = pl.ds(8 * r, 8), pl.ds(8 + 8 * r, 8)
        out_eta[to, :] = e[0, here, :] * (1.0 / SA)
        out_x[to, :] = x[0, here, :] * (1.0 / SB)
        out_y[to, :] = y[0, here, :] * (1.0 / SB)
    for copy in copies:
        copy.wait()


def paste_kernel(block_size, *refs):
    offsets, eta, rolled, arrived, out = refs
    gx, grid, _, _ = place_of(block_size)
    own_offset = offsets[grid]
    left_offset = jnp.where(gx >= 1, offsets[lax.div(jnp.maximum(gx - 1, 0), block_size)], 0)
    row = iota(eta.shape, 0)
    out[...] = jnp.where(
        row >= own_offset, rolled[...], jnp.where(row < left_offset, arrived[...], eta[...])
    )


def shape(*dims):
    return jax.ShapeDtypeStruct(dims, F32)


def params():
    return pltpu.CompilerParams(vmem_limit_bytes=48 * 1024 * 1024)


def shards(
    ocean_eta,
    ocean_mx,
    ocean_ny,
    ocean_depth,
    ocean_class,
    manning,
    fine_eta,
    fine_qx,
    fine_qy,
    fine_depth,
    fine_wet,
    fine_class,
    fine_offset,
):
    ocean_rows, ocean_cols = ocean_eta.shape
    rows, cols = fine_eta.shape
    own = cols // LANES
    gx_count = lax.axis_size("gx")
    block_size = min(16, gx_count // 2)
    pairs_only = block_size == 2
    fine = (fine_eta, fine_qx, fine_qy, fine_depth, fine_wet, fine_class)
    ocean = (ocean_eta, ocean_mx, ocean_ny, ocean_depth, ocean_class)

    def vmem(*dims, dtype=F32):
        return pltpu.VMEM(dims, dtype)

    count = 1 if pairs_only else 2
    both = 6 * own * REACH + 5 * ITERS
    gx_even, gx_odd = pl.pallas_call(
        functools.partial(pack_rows_kernel, pairs_only),
        out_shape=(shape(both, LANES), shape(5 * ITERS if pairs_only else both, LANES)),
        in_specs=[SMEM] + [ANY] * 11,
        out_specs=(VMEM,) * 2,
        scratch_shapes=[
            vmem(4, count, HALO, cols),
            vmem(2, count, HALO, cols, dtype=jnp.int32),
            vmem(4, ocean_rows, ocean_cols),
            vmem(ocean_rows, ocean_cols, dtype=jnp.int32),
            pltpu.SemaphoreType.DMA((6 * count + 5,)),
        ],
        name="pack_rows",
    )(manning, *fine, *ocean)
    gx_even = swap_even(gx_even, "gx")
    gx_odd = swap_odd(gx_odd, "gx")

    own_even, own_odd, strip = pl.pallas_call(
        prepare_kernel,
        out_shape=(shape(rows, LANES),) * 2 + (shape(6, rows, LANES),),
        in_specs=[SMEM] + [VMEM] * 11,
        out_specs=(VMEM,) * 3,
        compiler_params=params(),
        cost_estimate=pl.CostEstimate(flops=0, bytes_accessed=5_000_000, transcendentals=0),
        name="prepare",
    )(manning, *fine, *ocean)

    n = rows // 8 + (HALO // 8) * count
    gy_even, gy_odd = pl.pallas_call(
        functools.partial(pack_columns_kernel, pairs_only, own, ocean_rows),
        out_shape=(shape(8 * n, LANES),) * 2,
        in_specs=[VMEM] * 4,
        out_specs=(VMEM,) * 2,
        compiler_params=params(),
        name="pack_columns",
    )(own_even, own_odd, gx_even, gx_odd)
    gy_even = swap_even(gy_even, "gy")
    gy_odd = swap_odd(gy_odd, "gy")

    *inner, means = pl.pallas_call(
        functools.partial(interior_kernel, block_size),
        out_shape=(shape(rows, cols),) * 3 + (shape(ocean_rows, ocean_cols),),
        in_specs=[SMEM, SMEM] + [VMEM] * 9,
        out_specs=(VMEM,) * 4,
        scratch_shapes=[vmem(own, 8 * n + 16, LANES)] * 11 + [vmem(2, own, 8, LANES)],
        compiler_params=params(),
        cost_estimate=pl.CostEstimate(flops=0, bytes_accessed=20_000_000, transcendentals=0),
        name="interior",
    )(manning, fine_offset, *fine, ocean_mx, gx_even, gx_odd)

    *strips, rolled = pl.pallas_call(
        functools.partial(border_kernel, block_size, cols),
        out_shape=(shape(rows, LANES),) * 3 + (shape(ocean_rows, ocean_cols),),
        in_specs=[SMEM] + [VMEM] * 7,
        out_specs=(VMEM,) * 4,
        scratch_shapes=[vmem(1, 8 * n + 16, LANES)] * 11 + [vmem(2, 1, 8, LANES)],
        compiler_params=params(),
        name="border",
    )(fine_offset, strip, ocean_mx, gx_even, gx_odd, gy_even, gy_odd, means)
    arrived = lax.ppermute(rolled, "gx", [(i, i + 1) for i in range(gx_count - 1)])

    n = ocean_rows // 8 + 1
    feta, fqx, fqy, eta, mx, ny = pl.pallas_call(
        finish_kernel,
        out_shape=(shape(rows, cols),) * 3 + (shape(ocean_rows, ocean_cols),) * 3,
        in_specs=[SMEM] + [VMEM] * 15,
        out_specs=(ANY,) * 3 + (VMEM,) * 3,
        scratch_shapes=[vmem(3, rows, cols), pltpu.SemaphoreType.DMA((3,))] + [vmem(2, 8 * n + 16, LANES)] * 10,
        compiler_params=params(),
        cost_estimate=pl.CostEstimate(flops=0, bytes_accessed=5_000_000, transcendentals=0),
        name="finish",
    )(manning, *ocean, gy_even, gy_odd, gx_even, gx_odd, *inner, *strips)

    eta = pl.pallas_call(
        functools.partial(paste_kernel, block_size),
        out_shape=shape(ocean_rows, ocean_cols),
        in_specs=[SMEM] + [VMEM] * 3,
        out_specs=VMEM,
        compiler_params=params(),
        name="paste",
    )(fine_offset, eta, rolled, arrived)
    return (eta, mx, ny, feta, fqx, fqy)


def solution(mesh):
    tile = P(("scen", "gx"), "gy")
    in_specs = (tile,) * 5 + (P(),) + (tile,) * 6 + (P("scen"),)
    return jax.shard_map(shards, mesh=mesh, in_specs=in_specs, out_specs=(tile,) * 6, check_vma=False)
```

```python
import functools

import jax
import jax.numpy as jnp
from jax import lax
from jax.experimental import pallas as pl
from jax.experimental.pallas import tpu as pltpu
from jax.sharding import PartitionSpec as P

R = 3
ITERS = 4
FSTEPS = R * ITERS
COURANT = 0.45
FLOOR = 0.25
SA = COURANT**2 / 2
SB = COURANT**3 / 2
POWER = -7.0 / 3.0
TFLOOR = 2 * SA * FLOOR
KSCALE = 0.5 * COURANT * (2 * SA) ** (7.0 / 3.0) / SB
CLOSED = 3.0e38
LANES = 128
HALO = 16
OLANE = 6 * 16
REACH = FSTEPS
VMEM = pl.BlockSpec(memory_space=pltpu.VMEM)
SMEM = pl.BlockSpec(memory_space=pltpu.SMEM)
ANY = pl.BlockSpec(memory_space=pltpu.HBM)
F32 = jnp.float32


def swap_even(value, axis):
    count = lax.axis_size(axis)
    return lax.ppermute(value, axis, [(i, i ^ 1) for i in range(count) if i ^ 1 < count])


def swap_odd(value, axis):
    count = lax.axis_size(axis)
    pairs = [(i, ((i + 1) ^ 1) - 1) for i in range(1, count)]
    return lax.ppermute(value, axis, [(a, b) for a, b in pairs if b < count])


def friction(classes, table):
    result = jnp.full(classes.shape, table[0], F32)
    for level_id in range(1, table.shape[0]):
        result = jnp.where(classes == level_id, table[level_id], result)
    return result


def field_of(refs, f, rows, cols, table):
    value = refs[f][rows, cols]
    if f < 4:
        return value * (SA, SB, SB, SA)[f]
    return friction(value, table) if f == 4 else value.astype(F32)


def fine_fields(refs, rows, cols, table):
    eta, qx, qy, depth, wet, classes = refs
    return tuple(field_of((eta, qx, qy, depth, classes, wet), f, rows, cols, table) for f in range(6))


def ocean_field(refs, j, rows, cols, table):
    value = refs[j][rows, cols]
    return value * (SA, SB, SB, SA)[j] if j < 4 else friction(value, table)


def ocean_fields(refs, rows, cols, table):
    return tuple(ocean_field(refs, j, rows, cols, table) for j in range(5))


def roll_to(value, start, target):
    return pltpu.roll(value, (target - start) % LANES, 1)


def copy_in(pairs, sems):
    copies = [pltpu.make_async_copy(src, dst, sems.at[i]) for i, (src, dst) in enumerate(pairs)]
    for copy in copies:
        copy.start()
    for copy in copies:
        copy.wait()


def pack_rows_kernel(pairs_only, *refs):
    table, fine, ocean = refs[0], refs[1:7], refs[7:12]
    count = 1 if pairs_only else 2
    outs, ocean_out = refs[12 : 12 + count], refs[12 + count]
    held, held_int, ocean_in, ocean_class, sems = refs[13 + count :]
    rows, cols = fine[0].shape
    tiles = cols // LANES
    ocean_rows = ocean[0].shape[0]
    is_even = lax.rem(lax.axis_index("gx"), 2) == 0
    pairs = []
    for side in range(count):
        last = is_even if side == 0 else jnp.logical_not(is_even)
        at = pl.multiple_of(jnp.where(last, rows - HALO, 0), 8)
        for f in range(6):
            target = held.at[f, side] if f < 4 else held_int.at[f - 4, side]
            pairs.append((fine[f].at[pl.ds(at, HALO), :], target))
    for j in range(5):
        pairs.append((ocean[j], ocean_in.at[j] if j < 4 else ocean_class))
    copy_in(pairs, sems)

    for side, out in enumerate(outs):
        last = is_even if side == 0 else jnp.logical_not(is_even)
        sources = [held.at[f, side] for f in range(4)] + [held_int.at[f, side] for f in range(2)]
        for t in range(tiles):
            at_cols = pl.ds(t * LANES, LANES)
            low = fine_fields(sources, pl.ds(HALO - REACH, REACH), at_cols, table)
            top = fine_fields(sources, pl.ds(0, REACH), at_cols, table)
            for f in range(6):
                out[pl.ds((f * tiles + t) * REACH, REACH), :] = jnp.where(last, low[f], top[f])
    sources = [ocean_in.at[j] for j in range(4)] + [ocean_class]
    low = ocean_fields(sources, pl.ds(ocean_rows - ITERS, ITERS), pl.ds(0, LANES), table)
    top = ocean_fields(sources, pl.ds(0, ITERS), pl.ds(0, LANES), table)
    for j in range(5):
        outs[0][pl.ds(6 * tiles * REACH + j * ITERS, ITERS), :] = jnp.where(is_even, low[j], top[j])
        ocean_out[pl.ds(j * ITERS, ITERS), :] = jnp.where(is_even, top[j], low[j])


def halo_blocks(pairs_only, messages, block, gx_is_even):
    rows = [message[pl.ds(block * REACH, REACH), :] for message in messages]
    gap = jnp.zeros((HALO - REACH, LANES), F32)
    if pairs_only:
        return [jnp.where(gx_is_even, jnp.concatenate([rows[0], gap], 0), jnp.concatenate([gap, rows[0]], 0))]
    after = jnp.where(gx_is_even, rows[0], rows[1])
    before = jnp.where(gx_is_even, rows[1], rows[0])
    return [jnp.concatenate([after, gap], 0), jnp.concatenate([gap, before], 0)]


def ocean_halo(even, odd, gx_is_even):
    return jnp.where(gx_is_even, jnp.concatenate([even, odd], 0), jnp.concatenate([odd, even], 0))


def ocean_part(message, j):
    return message[pl.ds(message.shape[0] - (5 - j) * ITERS, ITERS), :]


def packed_columns(parts):
    lane = iota((8, LANES), 1)
    west = jnp.zeros((8, LANES), F32)
    east = jnp.zeros((8, LANES), F32)
    for at, wide, from_west, from_east in parts:
        inside = (lane >= at) & (lane < at + wide)
        west = jnp.where(inside, roll_to(from_west, 0, at), west)
        east = jnp.where(inside, roll_to(from_east, LANES - wide, at), east)
    is_even = lax.rem(lax.axis_index("gy"), 2) == 0
    return jnp.where(is_even, east, west), jnp.where(is_even, west, east)


def columns_parts(first, last, ocean_values):
    parts = [(16 * f, 16, first[f], last[f]) for f in range(6)]
    return parts + [(OLANE + ITERS * j, ITERS, v, v) for j, v in enumerate(ocean_values)]


def strip_lanes(first, last):
    lane = iota((8, LANES), 1)
    moved = jnp.where(lane < 64, roll_to(last, LANES - 32, 32), 0.0)
    return jnp.where(lane < 32, first, moved)


def pack_columns_kernel(pairs_only, tiles, ocean_rows, *refs):
    own, messages, outs = refs[:2], refs[2:-2], refs[-2:]
    rows = own[0].shape[0]
    gx_is_even = lax.rem(lax.axis_index("gx"), 2) == 0
    extra = pl.ds(ocean_rows, 8)
    gap = jnp.zeros((ITERS, LANES), F32)
    values = [ocean_halo(ocean_part(messages[0], j), gap, gx_is_even) for j in range(5)]
    parts = [(OLANE + ITERS * j, ITERS, v, v) for j, v in enumerate(values)]
    ocean_lanes = iota((8, LANES), 1) >= OLANE
    for out, mine, value in zip(outs, own, packed_columns(parts)):
        out[0:rows, :] = mine[...]
        out[extra, :] = jnp.where(ocean_lanes, value, mine[extra, :])
    halos = [
        [halo_blocks(pairs_only, messages, f * tiles + t, gx_is_even) for t in (0, tiles - 1)] for f in range(6)
    ]
    for r in range(rows // 8, outs[0].shape[0] // 8):
        side, half = divmod(r - rows // 8, HALO // 8)
        first, last = (
            [halos[f][end][side][8 * half : 8 * half + 8] for f in range(6)] for end in range(2)
        )
        for out, value in zip(outs, packed_columns(columns_parts(first, last, ()))):
            out[pl.ds(8 * r, 8), :] = value


def lane_next(values, ring=True):
    lane = lax.broadcasted_iota(jnp.int32, values[0].shape, 1)
    rolled = [pltpu.roll(v, LANES - 1, 1) for v in values]
    count = len(values)
    if count == 1:
        return rolled
    inner = [jnp.where(lane == LANES - 1, rolled[t + 1], rolled[t]) for t in range(count - 1)]
    end = jnp.where(lane == LANES - 1, rolled[0], rolled[-1]) if ring else rolled[-1]
    return inner + [end]


def lane_prev(values, ring=True):
    lane = lax.broadcasted_iota(jnp.int32, values[0].shape, 1)
    rolled = [pltpu.roll(v, 1, 1) for v in values]
    count = len(values)
    if count == 1:
        return rolled
    start = jnp.where(lane == 0, rolled[-1] if ring else 0.0, rolled[0])
    return [start] + [jnp.where(lane == 0, rolled[t - 1], rolled[t]) for t in range(1, count)]


def new_flux(flux, eta, eta_next, wet, wet_next, opened, drag):
    total = wet + wet_next
    power = jnp.exp2(POWER * jnp.log2(jnp.maximum(total, TFLOOR)))
    denom = opened + (drag * jnp.abs(flux)) * power
    return (flux - total * (eta_next - eta)) / denom


def prepare_faces(tiles, n, kf, wf, kx, ky, ox, oy, ring=True):
    for t in range(tiles):
        wrap = pl.ds(8 + 8 * n, 8)
        kf[t, wrap, :] = kf[t, pl.ds(8, 8), :]
        if wf is not None:
            wf[t, wrap, :] = wf[t, pl.ds(8, 8), :]
    for r in range(n):
        here, after = pl.ds(8 + 8 * r, 8), pl.ds(9 + 8 * r, 8)
        k = [kf[t, here, :] for t in range(tiles)]
        k_next = lane_next(k)
        if wf is not None:
            w = [wf[t, here, :] for t in range(tiles)]
            w_next = lane_next(w)
        for t in range(tiles):
            kx[t, here, :] = KSCALE * (k[t] + kf[t, after, :])
            ky[t, here, :] = KSCALE * (k[t] + k_next[t])
            if wf is not None:
                ox[t, here, :] = jnp.where(w[t] * wf[t, after, :] > 0.5, 1.0, CLOSED)
                open_y = w[t] * w_next[t] > 0.5
                if not ring and t == tiles - 1:
                    open_y = open_y & (iota((8, LANES), 1) < LANES - 1)
                oy[t, here, :] = jnp.where(open_y, 1.0, CLOSED)


def level_pass(tiles, n, e, g, x, y, d, ring=True):
    for r in range(n):
        here, before = pl.ds(8 + 8 * r, 8), pl.ds(7 + 8 * r, 8)
        south = [y[t, here, :] for t in range(tiles)]
        south_prev = lane_prev(south, ring)
        for t in range(tiles):
            flow = (x[t, here, :] - x[t, before, :]) + (south[t] - south_prev[t])
            eta = e[t, here, :] - flow
            wet = jnp.maximum(d[t, here, :] + eta, 0.0)
            e[t, here, :] = eta
            g[t, here, :] = wet
            if r == 0:
                e[t, pl.ds(8 + 8 * n, 8), :] = eta
                g[t, pl.ds(8 + 8 * n, 8), :] = wet


def flux_pass(tiles, n, e, g, x, y, kx, ky, ox, oy, fix, ring=True, ghost=True):
    for r in range(n):
        here, after = pl.ds(8 + 8 * r, 8), pl.ds(9 + 8 * r, 8)
        eta = [e[t, here, :] for t in range(tiles)]
        wet = [g[t, here, :] for t in range(tiles)]
        eta_next, wet_next = lane_next(eta, ring), lane_next(wet, ring)
        for t in range(tiles):
            fx = new_flux(
                x[t, here, :], eta[t], e[t, after, :], wet[t], g[t, after, :], ox[t, here, :], kx[t, here, :]
            )
            fx = fix(r, t, fx)
            x[t, here, :] = fx
            if ghost and r == n - 1:
                x[t, pl.ds(0, 8), :] = fx
            y[t, here, :] = new_flux(
                y[t, here, :], eta[t], eta_next[t], wet[t], wet_next[t], oy[t, here, :], ky[t, here, :]
            )


def dot(a, b):
    return lax.dot_general(
        a, b, (((1,), (0,)), ((), ())), precision=lax.Precision.HIGHEST, preferred_element_type=F32
    )


def iota(shape, dim):
    return lax.broadcasted_iota(jnp.int32, shape, dim)


def place_of(block_size):
    gx = lax.axis_index("gx")
    slot = lax.rem(gx, block_size)
    return gx, lax.div(gx, block_size), slot == 0, slot == block_size - 1


def grid_edges(ocean_mx, beyond, own_offset, ocean_rows, spread_to, wf, rows, edges):
    at = own_offset - 1
    own = [ocean_mx[pl.ds(at, 1), :] * SB, ocean_mx[ocean_rows - 1 : ocean_rows, :] * SB]
    source = [jnp.concatenate(own + own * 3, 0)]
    if beyond:
        picks = iota((8, ocean_rows), 1) == jnp.where(iota((8, ocean_rows), 0) == 0, at, ocean_rows - 1)
        source += [dot(picks.astype(F32), tile) for tile in beyond]
    source = jnp.concatenate(source, 1)
    spread = dot(source, spread_to.astype(F32))
    for t in range(edges.shape[1]):
        cut = spread[:, t * LANES : (t + 1) * LANES]
        wet_first = wf[t, pl.ds(8, 8), :]
        wet_last = wf[t, pl.ds(rows, 8), :]
        edges[0, t, :, :] = jnp.broadcast_to(cut[0:1, :] * wet_first[0:1, :], (8, LANES))
        edges[1, t, :, :] = jnp.broadcast_to(cut[1:2, :] * wet_last[7:8, :], (8, LANES))


def run_coastal(tiles, n, rows, first, last, state, edges, ring):
    e, g, x, y, d, kx, ky, ox, oy = state
    sub = iota((8, LANES), 0)
    ghost = n > rows // 8
    west_mask = (sub == 7) & first
    east_mask = (sub == 7) & last

    def fix(r, t, fx):
        if r == rows // 8 - 1:
            fx = jnp.where(east_mask, edges[1, t, :, :], fx)
        if ghost and r == n - 1:
            fx = jnp.where(west_mask, edges[0, t, :, :], fx)
        return fx

    for t in range(tiles):
        before = x[t, pl.ds(8 * n, 8), :] if ghost else 0.0
        x[t, pl.ds(0, 8), :] = jnp.where(west_mask, edges[0, t, :, :], before)

    def step(_, carry):
        level_pass(tiles, n, e, g, x, y, d, ring)
        flux_pass(tiles, n, e, g, x, y, kx, ky, ox, oy, fix, ring, ghost)
        return carry

    lax.fori_loop(0, FSTEPS, step, 0, unroll=4)


def interior_kernel(block_size, *refs):
    table, offsets, fine, ocean = refs[0], refs[1], refs[2:8], refs[8:13]
    outs, (even_out, odd_out, strip) = refs[13:16], refs[16:19]
    e, g, x, y, d, kf, wf, kx, ky, ox, oy, edges = refs[19:]
    ocean_mx = ocean[1]
    ocean_rows = ocean_mx.shape[0]
    rows, cols = fine[0].shape
    tiles = cols // LANES
    n = rows // 8
    gx, grid, first, last = place_of(block_size)
    dest = (e, x, y, d, kf, wf)
    for r in range(n):
        src, here = pl.ds(8 * r, 8), pl.ds(8 + 8 * r, 8)
        values = [fine_fields(fine, src, pl.ds(t * LANES, LANES), table) for t in range(tiles)]
        for t in range(tiles):
            for f in range(6):
                dest[f][t, here, :] = values[t][f]
        ocean_values = ocean_fields(ocean, src, pl.ds(0, LANES), table) if 8 * r < ocean_rows else ()
        even_out[src, :], odd_out[src, :] = packed_columns(columns_parts(values[0], values[-1], ocean_values))
        for f in range(6):
            strip[f, src, :] = strip_lanes(values[0][f], values[-1][f])

    spread_to = iota((LANES, cols), 0) == lax.div(iota((LANES, cols), 1), R)
    grid_edges(ocean_mx, [], offsets[grid], ocean_rows, spread_to, wf, rows, edges)
    prepare_faces(tiles, n, kf, wf, kx, ky, ox, oy, False)
    run_coastal(tiles, n, rows, first, last, (e, g, x, y, d, kx, ky, ox, oy), edges, False)
    for r in range(n):
        to, here = pl.ds(8 * r, 8), pl.ds(8 + 8 * r, 8)
        for t in range(tiles):
            at_cols = pl.ds(t * LANES, LANES)
            outs[0][to, at_cols] = e[t, here, :] * (1.0 / SA)
            outs[1][to, at_cols] = x[t, here, :] * (1.0 / SB)
            outs[2][to, at_cols] = y[t, here, :] * (1.0 / SB)


def rows_kernel(block_size, *refs):
    table, offsets, fine = refs[0], refs[1], refs[2:8]
    pairs_only = block_size == 2
    count = 1 if pairs_only else 2
    messages = refs[8 : 8 + count]
    inner = refs[8 + count : 11 + count]
    outs, out_means = refs[11 + count : 14 + count], refs[14 + count]
    e, g, x, y, d, kf, wf, kx, ky, ox, oy = refs[15 + count :]
    rows, cols = fine[0].shape
    ocean_rows = out_means.shape[0]
    tiles = cols // LANES
    near = 2 * REACH // 8
    n = near + HALO // 8
    gx, grid, first, last = place_of(block_size)
    gx_is_even = lax.rem(gx, 2) == 0
    sub = iota((8, LANES), 0)
    dest = (e, x, y, d, kf, wf)
    for i in range(3):
        outs[i][...] = inner[i][...]

    for side in range(count):
        to_next = gx_is_even if pairs_only else side == 0
        start = jnp.where(to_next, rows - 8 * near, 0) if pairs_only else (rows - 8 * near) * (side == 0)
        for r in range(near):
            src = pl.ds(pl.multiple_of(start + 8 * r, 8), 8) if pairs_only else pl.ds(start + 8 * r, 8)
            for t in range(tiles):
                for f, value in enumerate(fine_fields(fine, src, pl.ds(t * LANES, LANES), table)):
                    dest[f][t, pl.ds(8 + 8 * r, 8), :] = value
        for f in range(6):
            for t in range(tiles):
                block = halo_blocks(pairs_only, messages, f * tiles + t, gx_is_even)[side]
                dest[f][t, pl.ds(8 + 8 * near, HALO), :] = block
        prepare_faces(tiles, n, kf, wf, kx, ky, ox, oy, False)
        for t in range(tiles):
            x[t, pl.ds(0, 8), :] = x[t, pl.ds(8 * n, 8), :]

        def step(_, carry):
            level_pass(tiles, n, e, g, x, y, d, False)
            flux_pass(tiles, n, e, g, x, y, kx, ky, ox, oy, lambda r, t, fx: fx, False)
            return carry

        lax.fori_loop(0, FSTEPS, step, 0, unroll=4)

        open_end = jnp.logical_not(jnp.where(to_next, last, first))
        for half in range(2):
            if pairs_only:
                src = pl.multiple_of(jnp.where(to_next, 8 * (near - 2 + half), 8 * half), 8)
                to = pl.multiple_of(jnp.where(to_next, rows - HALO + 8 * half, 8 * half), 8)
            else:
                src = 8 * (near - 2 + half) if to_next else 8 * half
                to = rows - HALO + 8 * half if to_next else 8 * half
            depth_in = jnp.where(to_next, HALO - 1 - (sub + 8 * half), sub + 8 * half)
            take = (depth_in < FSTEPS) & open_end
            for i, (held, scale) in enumerate(((e, 1.0 / SA), (x, 1.0 / SB), (y, 1.0 / SB))):
                for t in range(tiles):
                    at_cols = pl.ds(t * LANES, LANES)
                    value = held[t, pl.ds(8 + src, 8), :] * scale
                    outs[i][pl.ds(to, 8), at_cols] = jnp.where(take, value, outs[i][pl.ds(to, 8), at_cols])

    gather_cols = (lax.div(iota((cols, LANES), 0), R) == iota((cols, LANES), 1)).astype(F32)
    out_means[...] = coarse_means(outs[0][...], gather_cols, offsets[grid], ocean_rows)


def coarse_means(eta, gather_cols, own_offset, ocean_rows):
    shape = (ocean_rows, eta.shape[0])
    coarse_row = lax.rem(lax.div(iota(shape, 1), R) + own_offset, ocean_rows)
    gather_rows = (coarse_row == iota(shape, 0)).astype(F32)
    return dot(dot(gather_rows, eta), gather_cols) * (1.0 / (R * R))


def border_kernel(block_size, cols, *refs):
    pairs_only = block_size == 2
    count = 1 if pairs_only else 2
    offsets, strip, ocean_mx, messages = refs[0], refs[1], refs[2], refs[3 : 3 + count]
    gy_even, gy_odd, ocean_odd, inner_means = refs[3 + count : 7 + count]
    outs, out_even, out_odd = refs[7 + count : 10 + count], refs[10 + count], refs[11 + count]
    e, g, x, y, d, kf, wf, kx, ky, ox, oy, edges = refs[12 + count :]
    rows = strip.shape[1]
    own = cols // LANES
    n = rows // 8 + (HALO // 8) * (1 if pairs_only else 2)
    gx, grid, first, last = place_of(block_size)
    gx_is_even = lax.rem(gx, 2) == 0
    gy_is_even = lax.rem(lax.axis_index("gy"), 2) == 0
    lane = iota((8, LANES), 1)
    dest = (e, x, y, d, kf, wf)
    halos = [
        [halo_blocks(pairs_only, messages, f * own + t, gx_is_even) for t in (0, own - 1)] for f in range(6)
    ]
    for r in range(n):
        src, here = pl.ds(8 * r, 8), pl.ds(8 + 8 * r, 8)
        if 8 * r < rows:
            mine = [strip[f, src, :] for f in range(6)]
        else:
            side, half = divmod(r - rows // 8, HALO // 8)
            cut = slice(8 * half, 8 * half + 8)
            mine = [strip_lanes(halos[f][0][side][cut], halos[f][1][side][cut]) for f in range(6)]
        from_even, from_odd = gy_even[src, :], gy_odd[src, :]
        from_east = jnp.where(gy_is_even, from_even, from_odd)
        from_west = jnp.where(gy_is_even, from_odd, from_even)
        for f in range(6):
            east = roll_to(from_east, 16 * f, 64)
            west = roll_to(from_west, 16 * f, LANES - 16)
            value = jnp.where((lane >= 64) & (lane < 80), east, mine[f])
            dest[f][0, here, :] = jnp.where(lane < LANES - 16, value, west)

    ocean_rows = ocean_mx.shape[0]
    from_even, from_odd = gy_even[0:ocean_rows, :], gy_odd[0:ocean_rows, :]
    from_east = jnp.where(gy_is_even, from_even, from_odd)
    from_west = jnp.where(gy_is_even, from_odd, from_even)
    lanes = iota((ocean_rows, LANES), 1)
    mx_halo = jnp.where(
        lanes < ITERS,
        roll_to(from_east, OLANE + ITERS, 0),
        roll_to(from_west, OLANE + ITERS, LANES - ITERS),
    )
    to = iota((2 * LANES, LANES), 1)
    wanted = jnp.where(to < 32, lax.div(to, R), lax.div(to + (cols - 64), R))
    wanted = jnp.where(to < 64, wanted, jnp.where(to < 80, LANES + lax.div(to - 64, R), 0))
    wanted = jnp.where(to < LANES - 16, wanted, 2 * LANES - 1 - lax.div(LANES - 1 - to, R))
    spread_to = iota((2 * LANES, LANES), 0) == wanted
    grid_edges(ocean_mx, [mx_halo], offsets[grid], ocean_rows, spread_to, wf, rows, edges)
    prepare_faces(1, n, kf, wf, kx, ky, ox, oy)
    run_coastal(1, n, rows, first, last, (e, g, x, y, d, kx, ky, ox, oy), edges, True)

    for i, (held, scale) in enumerate(((e, 1.0 / SA), (x, 1.0 / SB), (y, 1.0 / SB))):
        outs[i][...] = held[0, 8 : 8 + rows, :] * scale
    source, target = iota((LANES, LANES), 0), iota((LANES, LANES), 1)
    column = jnp.where(source < 32, source, source + (cols - 64))
    inside = (source < FSTEPS) | ((source >= 64 - FSTEPS) & (source < 64))
    gather = ((lax.div(column, R) == target) & inside).astype(F32)
    means = coarse_means(outs[0][...], gather, offsets[grid], ocean_rows)
    col = iota((ocean_rows, LANES), 1)
    means = jnp.where((col < ITERS) | (col >= LANES - ITERS), means, inner_means[...])
    out_even[...] = means
    out_odd[0:ocean_rows, :] = means
    out_odd[ocean_rows : ocean_rows + 5 * ITERS, :] = ocean_odd[...]
    for k, side in enumerate((gy_even, gy_odd)):
        corner = jnp.where(gx_is_even, side[0:ITERS, :], side[ocean_rows - ITERS : ocean_rows, :])
        out_odd[pl.ds(ocean_rows + (5 + k) * ITERS, ITERS), :] = corner


def finish_kernel(*refs):
    inner, strips, table, ocean = refs[0:3], refs[3:6], refs[6], refs[7:12]
    gy_even, gy_odd, gx_even = refs[12:15]
    outs, state, final, sems = refs[15:18], refs[18], refs[19], refs[20]
    rows, cols = final.shape[1:]
    own = cols // LANES
    lane = iota((8, LANES), 1)
    copies = [pltpu.make_async_copy(final.at[i], outs[i], sems.at[i]) for i in range(3)]
    for i in range(3):
        for r in range(rows // 8):
            to = pl.ds(8 * r, 8)
            value = strips[i][to, :]
            for t in range(own):
                at_cols = pl.ds(t * LANES, LANES)
                kept = inner[i][to, at_cols]
                if t == 0:
                    kept = jnp.where(lane < FSTEPS, value, kept)
                if t == own - 1:
                    kept = jnp.where(lane >= LANES - FSTEPS, roll_to(value, 32, LANES - 32), kept)
                final[i, to, at_cols] = kept
        copies[i].start()

    ocean_rows = ocean[0].shape[0]
    gx_is_even = lax.rem(lax.axis_index("gx"), 2) == 0
    for r in range(ocean_rows // 8):
        src = pl.ds(8 * r, 8)
        for j, value in enumerate(ocean_fields(ocean, src, pl.ds(0, LANES), table)):
            state[j, 0, src, :] = value
            state[j, 1, src, :] = unpack_ocean(gy_even[src, :], gy_odd[src, :], j)
    halo = pl.ds(ocean_rows, 8)
    gap = jnp.zeros((ITERS, LANES), F32)
    for j in range(5):
        state[j, 0, halo, :] = ocean_halo(ocean_part(gx_even, j), gap, gx_is_even)
        state[j, 1, halo, :] = unpack_ocean(gy_even[halo, :], gy_odd[halo, :], j)
    for copy in copies:
        copy.wait()


def unpack_ocean(from_even, from_odd, j):
    gy_is_even = lax.rem(lax.axis_index("gy"), 2) == 0
    lane = iota((8, LANES), 1)
    from_east = jnp.where(gy_is_even, from_even, from_odd)
    from_west = jnp.where(gy_is_even, from_odd, from_even)
    east = roll_to(from_east, OLANE + ITERS * j, 0)
    west = roll_to(from_west, OLANE + ITERS * j, LANES - ITERS)
    return jnp.where(lane < ITERS, east, jnp.where(lane >= LANES - ITERS, west, 0.0))


def ocean_kernel(block_size, *refs):
    offsets, state, rolled, got_even, got_odd = refs[:5]
    out_eta, out_x, out_y = refs[5:8]
    e, g, x, y, d, kf, kx, ky, ox, oy = refs[8:]
    rows, cols = out_eta.shape
    tiles = 2
    n = rows // 8 + 1
    gx, gy = lax.axis_index("gx"), lax.axis_index("gy")
    gx_is_even = lax.rem(gx, 2) == 0
    lane = iota((8, LANES), 1)
    sub = iota((8, LANES), 0)
    here = pl.ds(8 + rows, 8)
    gap = jnp.zeros((ITERS, LANES), F32)
    corners = [got_odd[pl.ds(rows + (5 + k) * ITERS, ITERS), :] for k in range(2)]
    corners = [ocean_halo(gap, corner, gx_is_even) for corner in corners]
    for j, field in enumerate((e, x, y, d, kf)):
        for t in range(tiles):
            field[t, 8 : 8 + rows + 8, :] = state[j, t]
        odd = ocean_halo(gap, got_odd[pl.ds(rows + j * ITERS, ITERS), :], gx_is_even)
        field[0, here, :] = field[0, here, :] + odd
        field[1, here, :] = field[1, here, :] + unpack_ocean(*corners, j)

    prepare_faces(tiles, n, kf, None, kx, ky, None, None)
    rows_total, cols_total = rows * lax.axis_size("gx"), cols * lax.axis_size("gy")
    for r in range(n):
        here = pl.ds(8 + 8 * r, 8)
        row = sub + 8 * r
        row = jnp.where(row >= rows + 4, row - (rows + 8), row) + gx * rows
        for t in range(tiles):
            col = lane if t == 0 else jnp.where(lane < 64, lane + LANES, lane - LANES)
            col = col + gy * cols
            ox[t, here, :] = jnp.where((row >= 0) & (row < rows_total - 1), 1.0, CLOSED)
            oy[t, here, :] = jnp.where((col >= 0) & (col < cols_total - 1), 1.0, CLOSED)
    for t in range(tiles):
        x[t, pl.ds(0, 8), :] = x[t, pl.ds(8 * n, 8), :]

    def step(_, carry):
        level_pass(tiles, n, e, g, x, y, d)
        flux_pass(tiles, n, e, g, x, y, kx, ky, ox, oy, lambda r, t, fx: fx)
        return carry

    lax.fori_loop(0, ITERS, step, 0, unroll=4)
    _, grid, _, _ = place_of(block_size)
    own_offset = offsets[grid]
    left_offset = jnp.where(gx >= 1, offsets[lax.div(jnp.maximum(gx - 1, 0), block_size)], 0)
    for r in range(rows // 8):
        to, here = pl.ds(8 * r, 8), pl.ds(8 + 8 * r, 8)
        row = sub + 8 * r
        arrived = jnp.where(gx_is_even, got_odd[to, :], got_even[to, :])
        level = jnp.where(row < left_offset, arrived, e[0, here, :] * (1.0 / SA))
        out_eta[to, :] = jnp.where(row >= own_offset, rolled[to, :], level)
        out_x[to, :] = x[0, here, :] * (1.0 / SB)
        out_y[to, :] = y[0, here, :] * (1.0 / SB)


def shape(*dims):
    return jax.ShapeDtypeStruct(dims, F32)


def params():
    return pltpu.CompilerParams(vmem_limit_bytes=48 * 1024 * 1024)


def shards(
    ocean_eta,
    ocean_mx,
    ocean_ny,
    ocean_depth,
    ocean_class,
    manning,
    fine_eta,
    fine_qx,
    fine_qy,
    fine_depth,
    fine_wet,
    fine_class,
    fine_offset,
):
    ocean_rows, ocean_cols = ocean_eta.shape
    rows, cols = fine_eta.shape
    own = cols // LANES
    gx_count = lax.axis_size("gx")
    block_size = min(16, gx_count // 2)
    pairs_only = block_size == 2
    fine = (fine_eta, fine_qx, fine_qy, fine_depth, fine_wet, fine_class)
    ocean = (ocean_eta, ocean_mx, ocean_ny, ocean_depth, ocean_class)

    def vmem(*dims, dtype=F32):
        return pltpu.VMEM(dims, dtype)

    count = 1 if pairs_only else 2
    fine_length, ocean_length = 6 * own * REACH, 5 * ITERS
    lengths = [fine_length + ocean_length, fine_length][:count] + [ocean_length]
    *gx_fine, ocean_odd = pl.pallas_call(
        functools.partial(pack_rows_kernel, pairs_only),
        out_shape=tuple(shape(length, LANES) for length in lengths),
        in_specs=[SMEM] + [ANY] * 11,
        out_specs=(VMEM,) * len(lengths),
        scratch_shapes=[
            vmem(4, count, HALO, cols),
            vmem(2, count, HALO, cols, dtype=jnp.int32),
            vmem(4, ocean_rows, ocean_cols),
            vmem(ocean_rows, ocean_cols, dtype=jnp.int32),
            pltpu.SemaphoreType.DMA((6 * count + 5,)),
        ],
        name="pack_rows",
    )(manning, *fine, *ocean)
    gx_fine = [swap(message, "gx") for swap, message in zip((swap_even, swap_odd), gx_fine)]

    *inner, own_even, own_odd, strip = pl.pallas_call(
        functools.partial(interior_kernel, block_size),
        out_shape=(shape(rows, cols),) * 3 + (shape(rows, LANES),) * 2 + (shape(6, rows, LANES),),
        in_specs=[SMEM, SMEM] + [VMEM] * 11,
        out_specs=(VMEM,) * 6,
        scratch_shapes=[vmem(own, rows + 16, LANES)] * 11 + [vmem(2, own, 8, LANES)],
        compiler_params=params(),
        cost_estimate=pl.CostEstimate(flops=0, bytes_accessed=20_000_000, transcendentals=0),
        name="interior",
    )(manning, fine_offset, *fine, *ocean)

    n = rows // 8 + (HALO // 8) * count
    gy_even, gy_odd = pl.pallas_call(
        functools.partial(pack_columns_kernel, pairs_only, own, ocean_rows),
        out_shape=(shape(8 * n, LANES),) * 2,
        in_specs=[VMEM] * (2 + count),
        out_specs=(VMEM,) * 2,
        compiler_params=params(),
        name="pack_columns",
    )(own_even, own_odd, *gx_fine)
    gy_even = swap_even(gy_even, "gy")
    gy_odd = swap_odd(gy_odd, "gy")

    *inner, means = pl.pallas_call(
        functools.partial(rows_kernel, block_size),
        out_shape=(shape(rows, cols),) * 3 + (shape(ocean_rows, ocean_cols),),
        in_specs=[SMEM, SMEM] + [VMEM] * (9 + count),
        out_specs=(VMEM,) * 4,
        scratch_shapes=[vmem(own, 2 * REACH + HALO + 16, LANES)] * 11,
        compiler_params=params(),
        cost_estimate=pl.CostEstimate(flops=0, bytes_accessed=10_000_000, transcendentals=0),
        name="rows",
    )(manning, fine_offset, *fine, *gx_fine, *inner)

    odd_length = ocean_rows + 7 * ITERS
    *strips, rolled, to_odd = pl.pallas_call(
        functools.partial(border_kernel, block_size, cols),
        out_shape=(shape(rows, LANES),) * 3 + (shape(ocean_rows, ocean_cols), shape(odd_length, LANES)),
        in_specs=[SMEM] + [VMEM] * (6 + count),
        out_specs=(VMEM,) * 5,
        scratch_shapes=[vmem(1, 8 * n + 16, LANES)] * 11 + [vmem(2, 1, 8, LANES)],
        compiler_params=params(),
        name="border",
    )(fine_offset, strip, ocean_mx, *gx_fine, gy_even, gy_odd, ocean_odd, means)
    got_even = swap_even(rolled, "gx")
    got_odd = swap_odd(to_odd, "gx")

    n = ocean_rows // 8 + 1
    feta, fqx, fqy, state = pl.pallas_call(
        finish_kernel,
        out_shape=(shape(rows, cols),) * 3 + (shape(5, 2, 8 * n, LANES),),
        in_specs=[VMEM] * 6 + [SMEM] + [VMEM] * 8,
        out_specs=(ANY,) * 3 + (VMEM,),
        scratch_shapes=[vmem(3, rows, cols), pltpu.SemaphoreType.DMA((3,))],
        compiler_params=params(),
        cost_estimate=pl.CostEstimate(flops=0, bytes_accessed=5_000_000, transcendentals=0),
        name="finish",
    )(*inner, *strips, manning, *ocean, gy_even, gy_odd, gx_fine[0])

    eta, mx, ny = pl.pallas_call(
        functools.partial(ocean_kernel, block_size),
        out_shape=(shape(ocean_rows, ocean_cols),) * 3,
        in_specs=[SMEM] + [VMEM] * 4,
        out_specs=(VMEM,) * 3,
        scratch_shapes=[vmem(2, 8 * n + 16, LANES)] * 10,
        compiler_params=params(),
        name="ocean",
    )(fine_offset, state, rolled, got_even, got_odd)
    return (eta, mx, ny, feta, fqx, fqy)


def solution(mesh):
    tile = P(("scen", "gx"), "gy")
    in_specs = (tile,) * 5 + (P(),) + (tile,) * 6 + (P("scen"),)
    return jax.shard_map(shards, mesh=mesh, in_specs=in_specs, out_specs=(tile,) * 6, check_vma=False)
```

```python
import functools

import jax
import jax.numpy as jnp
from jax import lax
from jax.experimental import pallas as pl
from jax.experimental.pallas import tpu as pltpu
from jax.sharding import PartitionSpec as P

R = 3
ITERS = 4
FSTEPS = R * ITERS
COURANT = 0.45
FLOOR = 0.25
SA = COURANT**2 / 2
SB = COURANT**3 / 2
POWER = -7.0 / 3.0
TFLOOR = 2 * SA * FLOOR
KSCALE = 0.5 * COURANT * (2 * SA) ** (7.0 / 3.0) / SB
CLOSED = 3.0e38
LANES = 128
HALO = 16
OLANE = 6 * 16
REACH = FSTEPS
VMEM = pl.BlockSpec(memory_space=pltpu.VMEM)
SMEM = pl.BlockSpec(memory_space=pltpu.SMEM)
ANY = pl.BlockSpec(memory_space=pltpu.HBM)
F32 = jnp.float32


def swap_even(value, axis):
    count = lax.axis_size(axis)
    return lax.ppermute(value, axis, [(i, i ^ 1) for i in range(count) if i ^ 1 < count])


def swap_odd(value, axis):
    count = lax.axis_size(axis)
    pairs = [(i, ((i + 1) ^ 1) - 1) for i in range(1, count)]
    return lax.ppermute(value, axis, [(a, b) for a, b in pairs if b < count])


def friction(classes, table):
    result = jnp.full(classes.shape, table[0], F32)
    for level_id in range(1, table.shape[0]):
        result = jnp.where(classes == level_id, table[level_id], result)
    return result


def field_of(refs, f, rows, cols, table):
    value = refs[f][rows, cols]
    if f < 4:
        return value * (SA, SB, SB, SA)[f]
    return friction(value, table) if f == 4 else value.astype(F32)


def fine_fields(refs, rows, cols, table):
    eta, qx, qy, depth, wet, classes = refs
    return tuple(field_of((eta, qx, qy, depth, classes, wet), f, rows, cols, table) for f in range(6))


def ocean_field(refs, j, rows, cols, table):
    value = refs[j][rows, cols]
    return value * (SA, SB, SB, SA)[j] if j < 4 else friction(value, table)


def ocean_fields(refs, rows, cols, table):
    return tuple(ocean_field(refs, j, rows, cols, table) for j in range(5))


def roll_to(value, start, target):
    return pltpu.roll(value, (target - start) % LANES, 1)


def copy_in(pairs, sems):
    copies = [pltpu.make_async_copy(src, dst, sems.at[i]) for i, (src, dst) in enumerate(pairs)]
    for copy in copies:
        copy.start()
    for copy in copies:
        copy.wait()


def pack_rows_kernel(pairs_only, *refs):
    table, fine, ocean = refs[0], refs[1:7], refs[7:12]
    count = 1 if pairs_only else 2
    outs, ocean_out = refs[12 : 12 + count], refs[12 + count]
    held, held_int, ocean_in, ocean_class, sems = refs[13 + count :]
    rows, cols = fine[0].shape
    tiles = cols // LANES
    ocean_rows = ocean[0].shape[0]
    is_even = lax.rem(lax.axis_index("gx"), 2) == 0
    pairs = []
    for side in range(count):
        last = is_even if side == 0 else jnp.logical_not(is_even)
        at = pl.multiple_of(jnp.where(last, rows - HALO, 0), 8)
        for f in range(6):
            target = held.at[f, side] if f < 4 else held_int.at[f - 4, side]
            pairs.append((fine[f].at[pl.ds(at, HALO), :], target))
    for j in range(5):
        pairs.append((ocean[j], ocean_in.at[j] if j < 4 else ocean_class))
    copy_in(pairs, sems)

    for side, out in enumerate(outs):
        last = is_even if side == 0 else jnp.logical_not(is_even)
        sources = [held.at[f, side] for f in range(4)] + [held_int.at[f, side] for f in range(2)]
        for t in range(tiles):
            at_cols = pl.ds(t * LANES, LANES)
            low = fine_fields(sources, pl.ds(HALO - REACH, REACH), at_cols, table)
            top = fine_fields(sources, pl.ds(0, REACH), at_cols, table)
            for f in range(6):
                out[pl.ds((f * tiles + t) * REACH, REACH), :] = jnp.where(last, low[f], top[f])
    sources = [ocean_in.at[j] for j in range(4)] + [ocean_class]
    low = ocean_fields(sources, pl.ds(ocean_rows - ITERS, ITERS), pl.ds(0, LANES), table)
    top = ocean_fields(sources, pl.ds(0, ITERS), pl.ds(0, LANES), table)
    for j in range(5):
        outs[0][pl.ds(6 * tiles * REACH + j * ITERS, ITERS), :] = jnp.where(is_even, low[j], top[j])
        ocean_out[pl.ds(j * ITERS, ITERS), :] = jnp.where(is_even, top[j], low[j])


def halo_blocks(pairs_only, messages, block, gx_is_even):
    rows = [message[pl.ds(block * REACH, REACH), :] for message in messages]
    gap = jnp.zeros((HALO - REACH, LANES), F32)
    if pairs_only:
        return [jnp.where(gx_is_even, jnp.concatenate([rows[0], gap], 0), jnp.concatenate([gap, rows[0]], 0))]
    after = jnp.where(gx_is_even, rows[0], rows[1])
    before = jnp.where(gx_is_even, rows[1], rows[0])
    return [jnp.concatenate([after, gap], 0), jnp.concatenate([gap, before], 0)]


def ocean_halo(even, odd, gx_is_even):
    return jnp.where(gx_is_even, jnp.concatenate([even, odd], 0), jnp.concatenate([odd, even], 0))


def ocean_part(message, j):
    return message[pl.ds(message.shape[0] - (5 - j) * ITERS, ITERS), :]


def packed_columns(parts):
    lane = iota((8, LANES), 1)
    west = jnp.zeros((8, LANES), F32)
    east = jnp.zeros((8, LANES), F32)
    for at, wide, from_west, from_east in parts:
        inside = (lane >= at) & (lane < at + wide)
        west = jnp.where(inside, roll_to(from_west, 0, at), west)
        east = jnp.where(inside, roll_to(from_east, LANES - wide, at), east)
    is_even = lax.rem(lax.axis_index("gy"), 2) == 0
    return jnp.where(is_even, east, west), jnp.where(is_even, west, east)


def columns_parts(first, last, ocean_values):
    parts = [(16 * f, 16, first[f], last[f]) for f in range(6)]
    return parts + [(OLANE + ITERS * j, ITERS, v, v) for j, v in enumerate(ocean_values)]


def strip_lanes(first, last):
    lane = iota((8, LANES), 1)
    moved = jnp.where(lane < 64, roll_to(last, LANES - 32, 32), 0.0)
    return jnp.where(lane < 32, first, moved)


def pack_columns_kernel(pairs_only, tiles, ocean_rows, *refs):
    own, messages, outs = refs[:2], refs[2:-2], refs[-2:]
    rows = own[0].shape[0]
    gx_is_even = lax.rem(lax.axis_index("gx"), 2) == 0
    extra = pl.ds(ocean_rows, 8)
    gap = jnp.zeros((ITERS, LANES), F32)
    values = [ocean_halo(ocean_part(messages[0], j), gap, gx_is_even) for j in range(5)]
    parts = [(OLANE + ITERS * j, ITERS, v, v) for j, v in enumerate(values)]
    ocean_lanes = iota((8, LANES), 1) >= OLANE
    for out, mine, value in zip(outs, own, packed_columns(parts)):
        out[0:rows, :] = mine[...]
        out[extra, :] = jnp.where(ocean_lanes, value, mine[extra, :])
    halos = [
        [halo_blocks(pairs_only, messages, f * tiles + t, gx_is_even) for t in (0, tiles - 1)] for f in range(6)
    ]
    for r in range(rows // 8, outs[0].shape[0] // 8):
        side, half = divmod(r - rows // 8, HALO // 8)
        first, last = (
            [halos[f][end][side][8 * half : 8 * half + 8] for f in range(6)] for end in range(2)
        )
        for out, value in zip(outs, packed_columns(columns_parts(first, last, ()))):
            out[pl.ds(8 * r, 8), :] = value


def lane_next(values, ring=True):
    lane = lax.broadcasted_iota(jnp.int32, values[0].shape, 1)
    rolled = [pltpu.roll(v, LANES - 1, 1) for v in values]
    count = len(values)
    if count == 1:
        return rolled
    inner = [jnp.where(lane == LANES - 1, rolled[t + 1], rolled[t]) for t in range(count - 1)]
    end = jnp.where(lane == LANES - 1, rolled[0], rolled[-1]) if ring else rolled[-1]
    return inner + [end]


def lane_prev(values, ring=True):
    lane = lax.broadcasted_iota(jnp.int32, values[0].shape, 1)
    rolled = [pltpu.roll(v, 1, 1) for v in values]
    count = len(values)
    if count == 1:
        return rolled
    start = jnp.where(lane == 0, rolled[-1] if ring else 0.0, rolled[0])
    return [start] + [jnp.where(lane == 0, rolled[t - 1], rolled[t]) for t in range(1, count)]


def new_flux(flux, eta, eta_next, wet, wet_next, opened, drag):
    total = wet + wet_next
    power = jnp.exp2(POWER * jnp.log2(jnp.maximum(total, TFLOOR)))
    denom = opened + (drag * jnp.abs(flux)) * power
    return (flux - total * (eta_next - eta)) / denom


def prepare_faces(tiles, n, kf, wf, kx, ky, ox, oy, ring=True):
    for t in range(tiles):
        wrap = pl.ds(8 + 8 * n, 8)
        kf[t, wrap, :] = kf[t, pl.ds(8, 8), :]
        if wf is not None:
            wf[t, wrap, :] = wf[t, pl.ds(8, 8), :]
    for r in range(n):
        here, after = pl.ds(8 + 8 * r, 8), pl.ds(9 + 8 * r, 8)
        k = [kf[t, here, :] for t in range(tiles)]
        k_next = lane_next(k)
        if wf is not None:
            w = [wf[t, here, :] for t in range(tiles)]
            w_next = lane_next(w)
        for t in range(tiles):
            kx[t, here, :] = KSCALE * (k[t] + kf[t, after, :])
            ky[t, here, :] = KSCALE * (k[t] + k_next[t])
            if wf is not None:
                ox[t, here, :] = jnp.where(w[t] * wf[t, after, :] > 0.5, 1.0, CLOSED)
                open_y = w[t] * w_next[t] > 0.5
                if not ring and t == tiles - 1:
                    open_y = open_y & (iota((8, LANES), 1) < LANES - 1)
                oy[t, here, :] = jnp.where(open_y, 1.0, CLOSED)


def level_pass(tiles, n, e, g, x, y, d, ring=True):
    for r in range(n):
        here, before = pl.ds(8 + 8 * r, 8), pl.ds(7 + 8 * r, 8)
        south = [y[t, here, :] for t in range(tiles)]
        south_prev = lane_prev(south, ring)
        for t in range(tiles):
            flow = (x[t, here, :] - x[t, before, :]) + (south[t] - south_prev[t])
            eta = e[t, here, :] - flow
            wet = jnp.maximum(d[t, here, :] + eta, 0.0)
            e[t, here, :] = eta
            g[t, here, :] = wet
            if r == 0:
                e[t, pl.ds(8 + 8 * n, 8), :] = eta
                g[t, pl.ds(8 + 8 * n, 8), :] = wet


def flux_pass(tiles, n, e, g, x, y, kx, ky, ox, oy, fix, ring=True, ghost=True):
    for r in range(n):
        here, after = pl.ds(8 + 8 * r, 8), pl.ds(9 + 8 * r, 8)
        eta = [e[t, here, :] for t in range(tiles)]
        wet = [g[t, here, :] for t in range(tiles)]
        eta_next, wet_next = lane_next(eta, ring), lane_next(wet, ring)
        for t in range(tiles):
            fx = new_flux(
                x[t, here, :], eta[t], e[t, after, :], wet[t], g[t, after, :], ox[t, here, :], kx[t, here, :]
            )
            fx = fix(r, t, fx)
            x[t, here, :] = fx
            if ghost and r == n - 1:
                x[t, pl.ds(0, 8), :] = fx
            y[t, here, :] = new_flux(
                y[t, here, :], eta[t], eta_next[t], wet[t], wet_next[t], oy[t, here, :], ky[t, here, :]
            )


def pieces(value):
    high = value.astype(jnp.bfloat16)
    rest = value - high.astype(F32)
    middle = rest.astype(jnp.bfloat16)
    return high, middle, (rest - middle.astype(F32)).astype(jnp.bfloat16)


def dot(a, b):
    return lax.dot_general(a, b, (((1,), (0,)), ((), ())), preferred_element_type=F32)


def pick_columns(value, picks):
    rows = value.shape[0]
    result = dot(jnp.concatenate(pieces(value), 0), picks.astype(jnp.bfloat16))
    return (result[2 * rows :] + result[rows : 2 * rows]) + result[:rows]


def pick_rows(picks, value):
    cols = value.shape[1]
    result = dot(picks.astype(jnp.bfloat16), jnp.concatenate(pieces(value), 1))
    return (result[:, 2 * cols :] + result[:, cols : 2 * cols]) + result[:, :cols]


def iota(shape, dim):
    return lax.broadcasted_iota(jnp.int32, shape, dim)


def place_of(block_size):
    gx = lax.axis_index("gx")
    slot = lax.rem(gx, block_size)
    return gx, lax.div(gx, block_size), slot == 0, slot == block_size - 1


def edge_rows(load, own_offset, ocean_rows):
    west, east = load(own_offset - 1), load(ocean_rows - 1)
    return jnp.concatenate([west, east] + [east] * 14, 0)


def grid_edges(sources, spread_to, wf, rows, edges):
    spread = pick_columns(jnp.concatenate(sources, 1), spread_to.astype(F32))
    for t in range(edges.shape[1]):
        cut = spread[:, t * LANES : (t + 1) * LANES]
        wet_first = wf[t, pl.ds(8, 8), :]
        wet_last = wf[t, pl.ds(rows, 8), :]
        edges[0, t, :, :] = jnp.broadcast_to(cut[0:1, :] * wet_first[0:1, :], (8, LANES))
        edges[1, t, :, :] = jnp.broadcast_to(cut[1:2, :] * wet_last[7:8, :], (8, LANES))


def run_coastal(tiles, n, rows, first, last, state, edges, ring, unroll):
    e, g, x, y, d, kx, ky, ox, oy = state
    sub = iota((8, LANES), 0)
    ghost = n > rows // 8
    west_mask = (sub == 7) & first
    east_mask = (sub == 7) & last

    def fix(r, t, fx):
        if r == rows // 8 - 1:
            fx = jnp.where(east_mask, edges[1, t, :, :], fx)
        if ghost and r == n - 1:
            fx = jnp.where(west_mask, edges[0, t, :, :], fx)
        return fx

    for t in range(tiles):
        before = x[t, pl.ds(8 * n, 8), :] if ghost else 0.0
        x[t, pl.ds(0, 8), :] = jnp.where(west_mask, edges[0, t, :, :], before)

    def step(_, carry):
        level_pass(tiles, n, e, g, x, y, d, ring)
        flux_pass(tiles, n, e, g, x, y, kx, ky, ox, oy, fix, ring, ghost)
        return carry

    lax.fori_loop(0, FSTEPS, step, 0, unroll=unroll)


def interior_kernel(block_size, *refs):
    table, offsets, fine, ocean = refs[0], refs[1], refs[2:8], refs[8:13]
    outs, (even_out, odd_out, strip) = refs[13:16], refs[16:19]
    e, g, x, y, d, kf, wf, kx, ky, ox, oy, edges = refs[19:]
    ocean_mx = ocean[1]
    ocean_rows = ocean_mx.shape[0]
    rows, cols = fine[0].shape
    tiles = cols // LANES
    n = rows // 8
    gx, grid, first, last = place_of(block_size)
    dest = (e, x, y, d, kf, wf)
    for r in range(n):
        src, here = pl.ds(8 * r, 8), pl.ds(8 + 8 * r, 8)
        values = [fine_fields(fine, src, pl.ds(t * LANES, LANES), table) for t in range(tiles)]
        for t in range(tiles):
            for f in range(6):
                dest[f][t, here, :] = values[t][f]
        ocean_values = ocean_fields(ocean, src, pl.ds(0, LANES), table) if 8 * r < ocean_rows else ()
        even_out[src, :], odd_out[src, :] = packed_columns(columns_parts(values[0], values[-1], ocean_values))
        for f in range(6):
            strip[f, src, :] = strip_lanes(values[0][f], values[-1][f])

    spread_to = iota((LANES, cols), 0) == lax.div(iota((LANES, cols), 1), R)
    sources = [edge_rows(lambda at: ocean_mx[pl.ds(at, 1), :] * SB, offsets[grid], ocean_rows)]
    grid_edges(sources, spread_to, wf, rows, edges)
    prepare_faces(tiles, n, kf, wf, kx, ky, ox, oy, False)
    run_coastal(tiles, n, rows, first, last, (e, g, x, y, d, kx, ky, ox, oy), edges, False, 4)
    for r in range(n):
        to, here = pl.ds(8 * r, 8), pl.ds(8 + 8 * r, 8)
        for t in range(tiles):
            at_cols = pl.ds(t * LANES, LANES)
            outs[0][to, at_cols] = e[t, here, :] * (1.0 / SA)
            outs[1][to, at_cols] = x[t, here, :] * (1.0 / SB)
            outs[2][to, at_cols] = y[t, here, :] * (1.0 / SB)


def rows_kernel(block_size, *refs):
    table, offsets, fine = refs[0], refs[1], refs[2:8]
    pairs_only = block_size == 2
    count = 1 if pairs_only else 2
    messages = refs[8 : 8 + count]
    inner = refs[8 + count : 11 + count]
    outs, out_means = refs[11 + count : 14 + count], refs[14 + count]
    e, g, x, y, d, kf, wf, kx, ky, ox, oy = refs[15 + count :]
    rows, cols = fine[0].shape
    ocean_rows = out_means.shape[0]
    tiles = cols // LANES
    near = 2 * REACH // 8
    n = near + HALO // 8
    gx, grid, first, last = place_of(block_size)
    gx_is_even = lax.rem(gx, 2) == 0
    sub = iota((8, LANES), 0)
    dest = (e, x, y, d, kf, wf)
    for i in range(3):
        outs[i][...] = inner[i][...]

    for side in range(count):
        to_next = gx_is_even if pairs_only else side == 0
        start = jnp.where(to_next, rows - 8 * near, 0) if pairs_only else (rows - 8 * near) * (side == 0)
        for r in range(near):
            src = pl.ds(pl.multiple_of(start + 8 * r, 8), 8) if pairs_only else pl.ds(start + 8 * r, 8)
            for t in range(tiles):
                for f, value in enumerate(fine_fields(fine, src, pl.ds(t * LANES, LANES), table)):
                    dest[f][t, pl.ds(8 + 8 * r, 8), :] = value
        for f in range(6):
            for t in range(tiles):
                block = halo_blocks(pairs_only, messages, f * tiles + t, gx_is_even)[side]
                dest[f][t, pl.ds(8 + 8 * near, HALO), :] = block
        prepare_faces(tiles, n, kf, wf, kx, ky, ox, oy, False)
        for t in range(tiles):
            x[t, pl.ds(0, 8), :] = x[t, pl.ds(8 * n, 8), :]

        def step(_, carry):
            level_pass(tiles, n, e, g, x, y, d, False)
            flux_pass(tiles, n, e, g, x, y, kx, ky, ox, oy, lambda r, t, fx: fx, False)
            return carry

        lax.fori_loop(0, FSTEPS, step, 0, unroll=FSTEPS)

        open_end = jnp.logical_not(jnp.where(to_next, last, first))
        for half in range(2):
            if pairs_only:
                src = pl.multiple_of(jnp.where(to_next, 8 * (near - 2 + half), 8 * half), 8)
                to = pl.multiple_of(jnp.where(to_next, rows - HALO + 8 * half, 8 * half), 8)
            else:
                src = 8 * (near - 2 + half) if to_next else 8 * half
                to = rows - HALO + 8 * half if to_next else 8 * half
            depth_in = jnp.where(to_next, HALO - 1 - (sub + 8 * half), sub + 8 * half)
            take = (depth_in < FSTEPS) & open_end
            for i, (held, scale) in enumerate(((e, 1.0 / SA), (x, 1.0 / SB), (y, 1.0 / SB))):
                for t in range(tiles):
                    at_cols = pl.ds(t * LANES, LANES)
                    value = held[t, pl.ds(8 + src, 8), :] * scale
                    outs[i][pl.ds(to, 8), at_cols] = jnp.where(take, value, outs[i][pl.ds(to, 8), at_cols])

    gather_cols = (lax.div(iota((cols, LANES), 0), R) == iota((cols, LANES), 1)).astype(F32)
    out_means[...] = coarse_means(outs[0][...], gather_cols, offsets[grid], ocean_rows)


def coarse_means(eta, gather_cols, own_offset, ocean_rows):
    shape = (ocean_rows, eta.shape[0])
    coarse_row = lax.rem(lax.div(iota(shape, 1), R) + own_offset, ocean_rows)
    gather_rows = (coarse_row == iota(shape, 0)).astype(F32)
    return pick_rows(gather_rows, pick_columns(eta, gather_cols)) * (1.0 / (R * R))


def border_kernel(block_size, cols, *refs):
    pairs_only = block_size == 2
    count = 1 if pairs_only else 2
    offsets, strip, ocean_mx, messages = refs[0], refs[1], refs[2], refs[3 : 3 + count]
    gy_even, gy_odd, ocean_odd, inner_means = refs[3 + count : 7 + count]
    outs, out_even, out_odd = refs[7 + count : 10 + count], refs[10 + count], refs[11 + count]
    e, g, x, y, d, kf, wf, kx, ky, ox, oy, edges = refs[12 + count :]
    rows = strip.shape[1]
    own = cols // LANES
    n = rows // 8 + (HALO // 8) * (1 if pairs_only else 2)
    gx, grid, first, last = place_of(block_size)
    gx_is_even = lax.rem(gx, 2) == 0
    gy_is_even = lax.rem(lax.axis_index("gy"), 2) == 0
    lane = iota((8, LANES), 1)
    dest = (e, x, y, d, kf, wf)
    halos = [
        [halo_blocks(pairs_only, messages, f * own + t, gx_is_even) for t in (0, own - 1)] for f in range(6)
    ]
    for r in range(n):
        src, here = pl.ds(8 * r, 8), pl.ds(8 + 8 * r, 8)
        if 8 * r < rows:
            mine = [strip[f, src, :] for f in range(6)]
        else:
            side, half = divmod(r - rows // 8, HALO // 8)
            cut = slice(8 * half, 8 * half + 8)
            mine = [strip_lanes(halos[f][0][side][cut], halos[f][1][side][cut]) for f in range(6)]
        from_even, from_odd = gy_even[src, :], gy_odd[src, :]
        from_east = jnp.where(gy_is_even, from_even, from_odd)
        from_west = jnp.where(gy_is_even, from_odd, from_even)
        for f in range(6):
            east = roll_to(from_east, 16 * f, 64)
            west = roll_to(from_west, 16 * f, LANES - 16)
            value = jnp.where((lane >= 64) & (lane < 80), east, mine[f])
            dest[f][0, here, :] = jnp.where(lane < LANES - 16, value, west)

    ocean_rows = ocean_mx.shape[0]
    from_even = edge_rows(lambda at: gy_even[pl.ds(at, 1), :], offsets[grid], ocean_rows)
    from_odd = edge_rows(lambda at: gy_odd[pl.ds(at, 1), :], offsets[grid], ocean_rows)
    from_east = jnp.where(gy_is_even, from_even, from_odd)
    from_west = jnp.where(gy_is_even, from_odd, from_even)
    mx_halo = jnp.where(
        iota((16, LANES), 1) < ITERS,
        roll_to(from_east, OLANE + ITERS, 0),
        roll_to(from_west, OLANE + ITERS, LANES - ITERS),
    )
    to = iota((2 * LANES, LANES), 1)
    wanted = jnp.where(to < 32, lax.div(to, R), lax.div(to + (cols - 64), R))
    wanted = jnp.where(to < 64, wanted, jnp.where(to < 80, LANES + lax.div(to - 64, R), 0))
    wanted = jnp.where(to < LANES - 16, wanted, 2 * LANES - 1 - lax.div(LANES - 1 - to, R))
    spread_to = iota((2 * LANES, LANES), 0) == wanted
    own_rows = edge_rows(lambda at: ocean_mx[pl.ds(at, 1), :] * SB, offsets[grid], ocean_rows)
    grid_edges([own_rows, mx_halo], spread_to, wf, rows, edges)
    prepare_faces(1, n, kf, wf, kx, ky, ox, oy)
    run_coastal(1, n, rows, first, last, (e, g, x, y, d, kx, ky, ox, oy), edges, True, FSTEPS)

    for i, (held, scale) in enumerate(((e, 1.0 / SA), (x, 1.0 / SB), (y, 1.0 / SB))):
        outs[i][...] = held[0, 8 : 8 + rows, :] * scale
    source, target = iota((LANES, LANES), 0), iota((LANES, LANES), 1)
    column = jnp.where(source < 32, source, source + (cols - 64))
    inside = (source < FSTEPS) | ((source >= 64 - FSTEPS) & (source < 64))
    gather = ((lax.div(column, R) == target) & inside).astype(F32)
    means = coarse_means(outs[0][...], gather, offsets[grid], ocean_rows)
    col = iota((ocean_rows, LANES), 1)
    means = jnp.where((col < ITERS) | (col >= LANES - ITERS), means, inner_means[...])
    out_even[...] = means
    out_odd[0:ocean_rows, :] = means
    out_odd[ocean_rows : ocean_rows + 5 * ITERS, :] = ocean_odd[...]
    for k, side in enumerate((gy_even, gy_odd)):
        corner = jnp.where(gx_is_even, side[0:ITERS, :], side[ocean_rows - ITERS : ocean_rows, :])
        out_odd[pl.ds(ocean_rows + (5 + k) * ITERS, ITERS), :] = corner


def finish_kernel(*refs):
    inner, strips, table, ocean = refs[0:3], refs[3:6], refs[6], refs[7:12]
    gy_even, gy_odd, gx_even = refs[12:15]
    outs, state, final, sems = refs[15:18], refs[18], refs[19], refs[20]
    rows, cols = final.shape[1:]
    own = cols // LANES
    lane = iota((8, LANES), 1)
    copies = [pltpu.make_async_copy(final.at[i], outs[i], sems.at[i]) for i in range(3)]
    for i in range(3):
        for r in range(rows // 8):
            to = pl.ds(8 * r, 8)
            value = strips[i][to, :]
            for t in range(own):
                at_cols = pl.ds(t * LANES, LANES)
                kept = inner[i][to, at_cols]
                if t == 0:
                    kept = jnp.where(lane < FSTEPS, value, kept)
                if t == own - 1:
                    kept = jnp.where(lane >= LANES - FSTEPS, roll_to(value, 32, LANES - 32), kept)
                final[i, to, at_cols] = kept
        copies[i].start()

    ocean_rows = ocean[0].shape[0]
    gx_is_even = lax.rem(lax.axis_index("gx"), 2) == 0
    for r in range(ocean_rows // 8):
        src = pl.ds(8 * r, 8)
        for j, value in enumerate(ocean_fields(ocean, src, pl.ds(0, LANES), table)):
            state[j, 0, src, :] = value
            state[j, 1, src, :] = unpack_ocean(gy_even[src, :], gy_odd[src, :], j)
    halo = pl.ds(ocean_rows, 8)
    gap = jnp.zeros((ITERS, LANES), F32)
    for j in range(5):
        state[j, 0, halo, :] = ocean_halo(ocean_part(gx_even, j), gap, gx_is_even)
        state[j, 1, halo, :] = unpack_ocean(gy_even[halo, :], gy_odd[halo, :], j)
    for copy in copies:
        copy.wait()


def unpack_ocean(from_even, from_odd, j):
    gy_is_even = lax.rem(lax.axis_index("gy"), 2) == 0
    lane = iota((8, LANES), 1)
    from_east = jnp.where(gy_is_even, from_even, from_odd)
    from_west = jnp.where(gy_is_even, from_odd, from_even)
    east = roll_to(from_east, OLANE + ITERS * j, 0)
    west = roll_to(from_west, OLANE + ITERS * j, LANES - ITERS)
    return jnp.where(lane < ITERS, east, jnp.where(lane >= LANES - ITERS, west, 0.0))


def ocean_kernel(block_size, *refs):
    offsets, state, rolled, got_even, got_odd = refs[:5]
    out_eta, out_x, out_y = refs[5:8]
    e, g, x, y, d, kf, kx, ky, ox, oy = refs[8:]
    rows, cols = out_eta.shape
    tiles = 2
    n = rows // 8 + 1
    gx, gy = lax.axis_index("gx"), lax.axis_index("gy")
    gx_is_even = lax.rem(gx, 2) == 0
    lane = iota((8, LANES), 1)
    sub = iota((8, LANES), 0)
    here = pl.ds(8 + rows, 8)
    gap = jnp.zeros((ITERS, LANES), F32)
    corners = [got_odd[pl.ds(rows + (5 + k) * ITERS, ITERS), :] for k in range(2)]
    corners = [ocean_halo(gap, corner, gx_is_even) for corner in corners]
    for j, field in enumerate((e, x, y, d, kf)):
        for t in range(tiles):
            field[t, 8 : 8 + rows + 8, :] = state[j, t]
        odd = ocean_halo(gap, got_odd[pl.ds(rows + j * ITERS, ITERS), :], gx_is_even)
        field[0, here, :] = field[0, here, :] + odd
        field[1, here, :] = field[1, here, :] + unpack_ocean(*corners, j)

    prepare_faces(tiles, n, kf, None, kx, ky, None, None)
    rows_total, cols_total = rows * lax.axis_size("gx"), cols * lax.axis_size("gy")
    for r in range(n):
        here = pl.ds(8 + 8 * r, 8)
        row = sub + 8 * r
        row = jnp.where(row >= rows + 4, row - (rows + 8), row) + gx * rows
        for t in range(tiles):
            col = lane if t == 0 else jnp.where(lane < 64, lane + LANES, lane - LANES)
            col = col + gy * cols
            ox[t, here, :] = jnp.where((row >= 0) & (row < rows_total - 1), 1.0, CLOSED)
            oy[t, here, :] = jnp.where((col >= 0) & (col < cols_total - 1), 1.0, CLOSED)
    for t in range(tiles):
        x[t, pl.ds(0, 8), :] = x[t, pl.ds(8 * n, 8), :]

    def step(_, carry):
        level_pass(tiles, n, e, g, x, y, d)
        flux_pass(tiles, n, e, g, x, y, kx, ky, ox, oy, lambda r, t, fx: fx)
        return carry

    lax.fori_loop(0, ITERS, step, 0, unroll=4)
    _, grid, _, _ = place_of(block_size)
    own_offset = offsets[grid]
    left_offset = jnp.where(gx >= 1, offsets[lax.div(jnp.maximum(gx - 1, 0), block_size)], 0)
    for r in range(rows // 8):
        to, here = pl.ds(8 * r, 8), pl.ds(8 + 8 * r, 8)
        row = sub + 8 * r
        arrived = jnp.where(gx_is_even, got_odd[to, :], got_even[to, :])
        level = jnp.where(row < left_offset, arrived, e[0, here, :] * (1.0 / SA))
        out_eta[to, :] = jnp.where(row >= own_offset, rolled[to, :], level)
        out_x[to, :] = x[0, here, :] * (1.0 / SB)
        out_y[to, :] = y[0, here, :] * (1.0 / SB)


def shape(*dims):
    return jax.ShapeDtypeStruct(dims, F32)


def params():
    return pltpu.CompilerParams(vmem_limit_bytes=48 * 1024 * 1024)


def shards(
    ocean_eta,
    ocean_mx,
    ocean_ny,
    ocean_depth,
    ocean_class,
    manning,
    fine_eta,
    fine_qx,
    fine_qy,
    fine_depth,
    fine_wet,
    fine_class,
    fine_offset,
):
    ocean_rows, ocean_cols = ocean_eta.shape
    rows, cols = fine_eta.shape
    own = cols // LANES
    gx_count = lax.axis_size("gx")
    block_size = min(16, gx_count // 2)
    pairs_only = block_size == 2
    fine = (fine_eta, fine_qx, fine_qy, fine_depth, fine_wet, fine_class)
    ocean = (ocean_eta, ocean_mx, ocean_ny, ocean_depth, ocean_class)

    def vmem(*dims, dtype=F32):
        return pltpu.VMEM(dims, dtype)

    count = 1 if pairs_only else 2
    fine_length, ocean_length = 6 * own * REACH, 5 * ITERS
    lengths = [fine_length + ocean_length, fine_length][:count] + [ocean_length]
    *gx_fine, ocean_odd = pl.pallas_call(
        functools.partial(pack_rows_kernel, pairs_only),
        out_shape=tuple(shape(length, LANES) for length in lengths),
        in_specs=[SMEM] + [ANY] * 11,
        out_specs=(VMEM,) * len(lengths),
        scratch_shapes=[
            vmem(4, count, HALO, cols),
            vmem(2, count, HALO, cols, dtype=jnp.int32),
            vmem(4, ocean_rows, ocean_cols),
            vmem(ocean_rows, ocean_cols, dtype=jnp.int32),
            pltpu.SemaphoreType.DMA((6 * count + 5,)),
        ],
        name="pack_rows",
    )(manning, *fine, *ocean)
    gx_fine = [swap(message, "gx") for swap, message in zip((swap_even, swap_odd), gx_fine)]

    *inner, own_even, own_odd, strip = pl.pallas_call(
        functools.partial(interior_kernel, block_size),
        out_shape=(shape(rows, cols),) * 3 + (shape(rows, LANES),) * 2 + (shape(6, rows, LANES),),
        in_specs=[SMEM, SMEM] + [VMEM] * 11,
        out_specs=(VMEM,) * 6,
        scratch_shapes=[vmem(own, rows + 16, LANES)] * 11 + [vmem(2, own, 8, LANES)],
        compiler_params=params(),
        cost_estimate=pl.CostEstimate(flops=0, bytes_accessed=20_000_000, transcendentals=0),
        name="interior",
    )(manning, fine_offset, *fine, *ocean)

    n = rows // 8 + (HALO // 8) * count
    gy_even, gy_odd = pl.pallas_call(
        functools.partial(pack_columns_kernel, pairs_only, own, ocean_rows),
        out_shape=(shape(8 * n, LANES),) * 2,
        in_specs=[VMEM] * (2 + count),
        out_specs=(VMEM,) * 2,
        compiler_params=params(),
        name="pack_columns",
    )(own_even, own_odd, *gx_fine)
    gy_even = swap_even(gy_even, "gy")
    gy_odd = swap_odd(gy_odd, "gy")

    *inner, means = pl.pallas_call(
        functools.partial(rows_kernel, block_size),
        out_shape=(shape(rows, cols),) * 3 + (shape(ocean_rows, ocean_cols),),
        in_specs=[SMEM, SMEM] + [VMEM] * (9 + count),
        out_specs=(VMEM,) * 4,
        scratch_shapes=[vmem(own, 2 * REACH + HALO + 16, LANES)] * 11,
        compiler_params=params(),
        cost_estimate=pl.CostEstimate(flops=0, bytes_accessed=10_000_000, transcendentals=0),
        name="rows",
    )(manning, fine_offset, *fine, *gx_fine, *inner)

    odd_length = ocean_rows + 7 * ITERS
    *strips, rolled, to_odd = pl.pallas_call(
        functools.partial(border_kernel, block_size, cols),
        out_shape=(shape(rows, LANES),) * 3 + (shape(ocean_rows, ocean_cols), shape(odd_length, LANES)),
        in_specs=[SMEM] + [VMEM] * (6 + count),
        out_specs=(VMEM,) * 5,
        scratch_shapes=[vmem(1, 8 * n + 16, LANES)] * 11 + [vmem(2, 1, 8, LANES)],
        compiler_params=params(),
        name="border",
    )(fine_offset, strip, ocean_mx, *gx_fine, gy_even, gy_odd, ocean_odd, means)
    got_even = swap_even(rolled, "gx")
    got_odd = swap_odd(to_odd, "gx")

    n = ocean_rows // 8 + 1
    feta, fqx, fqy, state = pl.pallas_call(
        finish_kernel,
        out_shape=(shape(rows, cols),) * 3 + (shape(5, 2, 8 * n, LANES),),
        in_specs=[VMEM] * 6 + [SMEM] + [VMEM] * 8,
        out_specs=(ANY,) * 3 + (VMEM,),
        scratch_shapes=[vmem(3, rows, cols), pltpu.SemaphoreType.DMA((3,))],
        compiler_params=params(),
        cost_estimate=pl.CostEstimate(flops=0, bytes_accessed=5_000_000, transcendentals=0),
        name="finish",
    )(*inner, *strips, manning, *ocean, gy_even, gy_odd, gx_fine[0])

    eta, mx, ny = pl.pallas_call(
        functools.partial(ocean_kernel, block_size),
        out_shape=(shape(ocean_rows, ocean_cols),) * 3,
        in_specs=[SMEM] + [VMEM] * 4,
        out_specs=(VMEM,) * 3,
        scratch_shapes=[vmem(2, 8 * n + 16, LANES)] * 10,
        compiler_params=params(),
        name="ocean",
    )(fine_offset, state, rolled, got_even, got_odd)
    return (eta, mx, ny, feta, fqx, fqy)


def solution(mesh):
    tile = P(("scen", "gx"), "gy")
    in_specs = (tile,) * 5 + (P(),) + (tile,) * 6 + (P("scen"),)
    return jax.shard_map(shards, mesh=mesh, in_specs=in_specs, out_specs=(tile,) * 6, check_vma=False)
```

```python
import functools

import jax
import jax.numpy as jnp
from jax import lax
from jax.experimental import pallas as pl
from jax.experimental.pallas import tpu as pltpu
from jax.sharding import PartitionSpec as P

R = 3
ITERS = 4
FSTEPS = R * ITERS
COURANT = 0.45
FLOOR = 0.25
SA = COURANT**2 / 2
SB = COURANT**3 / 2
POWER = -7.0 / 3.0
TFLOOR = 2 * SA * FLOOR
KSCALE = 0.5 * COURANT * (2 * SA) ** (7.0 / 3.0) / SB
CLOSED = 3.0e38
LANES = 128
HALO = 16
OLANE = 6 * 16
REACH = FSTEPS
VMEM = pl.BlockSpec(memory_space=pltpu.VMEM)
SMEM = pl.BlockSpec(memory_space=pltpu.SMEM)
ANY = pl.BlockSpec(memory_space=pltpu.HBM)
F32 = jnp.float32


def swap_even(value, axis):
    count = lax.axis_size(axis)
    return lax.ppermute(value, axis, [(i, i ^ 1) for i in range(count) if i ^ 1 < count])


def swap_odd(value, axis):
    count = lax.axis_size(axis)
    pairs = [(i, ((i + 1) ^ 1) - 1) for i in range(1, count)]
    return lax.ppermute(value, axis, [(a, b) for a, b in pairs if b < count])


def friction(classes, table):
    result = jnp.full(classes.shape, table[0], F32)
    for level_id in range(1, table.shape[0]):
        result = jnp.where(classes == level_id, table[level_id], result)
    return result


def field_of(refs, f, rows, cols, table):
    value = refs[f][rows, cols]
    if f < 4:
        return value * (SA, SB, SB, SA)[f]
    return friction(value, table) if f == 4 else value.astype(F32)


def fine_fields(refs, rows, cols, table):
    eta, qx, qy, depth, wet, classes = refs
    return tuple(field_of((eta, qx, qy, depth, classes, wet), f, rows, cols, table) for f in range(6))


def ocean_field(refs, j, rows, cols, table):
    value = refs[j][rows, cols]
    return value * (SA, SB, SB, SA)[j] if j < 4 else friction(value, table)


def ocean_fields(refs, rows, cols, table):
    return tuple(ocean_field(refs, j, rows, cols, table) for j in range(5))


def roll_to(value, start, target):
    return pltpu.roll(value, (target - start) % LANES, 1)


def copy_in(pairs, sems):
    copies = [pltpu.make_async_copy(src, dst, sems.at[i]) for i, (src, dst) in enumerate(pairs)]
    for copy in copies:
        copy.start()
    for copy in copies:
        copy.wait()


def pack_rows_kernel(pairs_only, *refs):
    table, fine, ocean = refs[0], refs[1:7], refs[7:12]
    count = 1 if pairs_only else 2
    outs, ocean_out = refs[12 : 12 + count], refs[12 + count]
    held, held_int, ocean_in, ocean_class, sems = refs[13 + count :]
    rows, cols = fine[0].shape
    tiles = cols // LANES
    ocean_rows = ocean[0].shape[0]
    is_even = lax.rem(lax.axis_index("gx"), 2) == 0
    pairs = []
    for side in range(count):
        last = is_even if side == 0 else jnp.logical_not(is_even)
        at = pl.multiple_of(jnp.where(last, rows - HALO, 0), 8)
        for f in range(6):
            target = held.at[f, side] if f < 4 else held_int.at[f - 4, side]
            pairs.append((fine[f].at[pl.ds(at, HALO), :], target))
    for j in range(5):
        pairs.append((ocean[j], ocean_in.at[j] if j < 4 else ocean_class))
    copy_in(pairs, sems)

    for side, out in enumerate(outs):
        last = is_even if side == 0 else jnp.logical_not(is_even)
        sources = [held.at[f, side] for f in range(4)] + [held_int.at[f, side] for f in range(2)]
        for t in range(tiles):
            at_cols = pl.ds(t * LANES, LANES)
            low = fine_fields(sources, pl.ds(HALO - REACH, REACH), at_cols, table)
            top = fine_fields(sources, pl.ds(0, REACH), at_cols, table)
            for f in range(6):
                out[pl.ds((f * tiles + t) * REACH, REACH), :] = jnp.where(last, low[f], top[f])
    sources = [ocean_in.at[j] for j in range(4)] + [ocean_class]
    low = ocean_fields(sources, pl.ds(ocean_rows - ITERS, ITERS), pl.ds(0, LANES), table)
    top = ocean_fields(sources, pl.ds(0, ITERS), pl.ds(0, LANES), table)
    for j in range(5):
        outs[0][pl.ds(6 * tiles * REACH + j * ITERS, ITERS), :] = jnp.where(is_even, low[j], top[j])
        ocean_out[pl.ds(j * ITERS, ITERS), :] = jnp.where(is_even, top[j], low[j])


def halo_blocks(pairs_only, messages, block, gx_is_even):
    rows = [message[pl.ds(block * REACH, REACH), :] for message in messages]
    gap = jnp.zeros((HALO - REACH, LANES), F32)
    if pairs_only:
        return [jnp.where(gx_is_even, jnp.concatenate([rows[0], gap], 0), jnp.concatenate([gap, rows[0]], 0))]
    after = jnp.where(gx_is_even, rows[0], rows[1])
    before = jnp.where(gx_is_even, rows[1], rows[0])
    return [jnp.concatenate([after, gap], 0), jnp.concatenate([gap, before], 0)]


def ocean_halo(even, odd, gx_is_even):
    return jnp.where(gx_is_even, jnp.concatenate([even, odd], 0), jnp.concatenate([odd, even], 0))


def ocean_part(message, j):
    return message[pl.ds(message.shape[0] - (5 - j) * ITERS, ITERS), :]


def packed_columns(parts):
    lane = iota((8, LANES), 1)
    west = jnp.zeros((8, LANES), F32)
    east = jnp.zeros((8, LANES), F32)
    for at, wide, from_west, from_east in parts:
        inside = (lane >= at) & (lane < at + wide)
        west = jnp.where(inside, roll_to(from_west, 0, at), west)
        east = jnp.where(inside, roll_to(from_east, LANES - wide, at), east)
    is_even = lax.rem(lax.axis_index("gy"), 2) == 0
    return jnp.where(is_even, east, west), jnp.where(is_even, west, east)


def columns_parts(first, last, ocean_values):
    parts = [(16 * f, 16, first[f], last[f]) for f in range(6)]
    return parts + [(OLANE + ITERS * j, ITERS, v, v) for j, v in enumerate(ocean_values)]


def strip_lanes(first, last):
    lane = iota((8, LANES), 1)
    moved = jnp.where(lane < 64, roll_to(last, LANES - 32, 32), 0.0)
    return jnp.where(lane < 32, first, moved)


def pack_columns_kernel(pairs_only, tiles, ocean_rows, *refs):
    own, messages, outs = refs[:2], refs[2:-2], refs[-2:]
    rows = own[0].shape[0]
    gx_is_even = lax.rem(lax.axis_index("gx"), 2) == 0
    extra = pl.ds(ocean_rows, 8)
    gap = jnp.zeros((ITERS, LANES), F32)
    values = [ocean_halo(ocean_part(messages[0], j), gap, gx_is_even) for j in range(5)]
    parts = [(OLANE + ITERS * j, ITERS, v, v) for j, v in enumerate(values)]
    ocean_lanes = iota((8, LANES), 1) >= OLANE
    for out, mine, value in zip(outs, own, packed_columns(parts)):
        out[0:rows, :] = mine[...]
        out[extra, :] = jnp.where(ocean_lanes, value, mine[extra, :])
    halos = [
        [halo_blocks(pairs_only, messages, f * tiles + t, gx_is_even) for t in (0, tiles - 1)] for f in range(6)
    ]
    for r in range(rows // 8, outs[0].shape[0] // 8):
        side, half = divmod(r - rows // 8, HALO // 8)
        first, last = (
            [halos[f][end][side][8 * half : 8 * half + 8] for f in range(6)] for end in range(2)
        )
        for out, value in zip(outs, packed_columns(columns_parts(first, last, ()))):
            out[pl.ds(8 * r, 8), :] = value


def lane_next(values, ring=True):
    lane = lax.broadcasted_iota(jnp.int32, values[0].shape, 1)
    rolled = [pltpu.roll(v, LANES - 1, 1) for v in values]
    count = len(values)
    if count == 1:
        return rolled
    inner = [jnp.where(lane == LANES - 1, rolled[t + 1], rolled[t]) for t in range(count - 1)]
    end = jnp.where(lane == LANES - 1, rolled[0], rolled[-1]) if ring else rolled[-1]
    return inner + [end]


def lane_prev(values, ring=True):
    lane = lax.broadcasted_iota(jnp.int32, values[0].shape, 1)
    rolled = [pltpu.roll(v, 1, 1) for v in values]
    count = len(values)
    if count == 1:
        return rolled
    start = jnp.where(lane == 0, rolled[-1] if ring else 0.0, rolled[0])
    return [start] + [jnp.where(lane == 0, rolled[t - 1], rolled[t]) for t in range(1, count)]


def new_flux(flux, eta, eta_next, wet, wet_next, opened, drag):
    total = wet + wet_next
    power = jnp.exp2(POWER * jnp.log2(jnp.maximum(total, TFLOOR)))
    denom = opened + (drag * jnp.abs(flux)) * power
    return (flux - total * (eta_next - eta)) / denom


def prepare_faces(tiles, n, kf, wf, kx, ky, ox, oy, ring=True):
    for t in range(tiles):
        wrap = pl.ds(8 + 8 * n, 8)
        kf[t, wrap, :] = kf[t, pl.ds(8, 8), :]
        if wf is not None:
            wf[t, wrap, :] = wf[t, pl.ds(8, 8), :]
    for r in range(n):
        here, after = pl.ds(8 + 8 * r, 8), pl.ds(9 + 8 * r, 8)
        k = [kf[t, here, :] for t in range(tiles)]
        k_next = lane_next(k)
        if wf is not None:
            w = [wf[t, here, :] for t in range(tiles)]
            w_next = lane_next(w)
        for t in range(tiles):
            kx[t, here, :] = KSCALE * (k[t] + kf[t, after, :])
            ky[t, here, :] = KSCALE * (k[t] + k_next[t])
            if wf is not None:
                ox[t, here, :] = jnp.where(w[t] * wf[t, after, :] > 0.5, 1.0, CLOSED)
                open_y = w[t] * w_next[t] > 0.5
                if not ring and t == tiles - 1:
                    open_y = open_y & (iota((8, LANES), 1) < LANES - 1)
                oy[t, here, :] = jnp.where(open_y, 1.0, CLOSED)


def level_pass(tiles, n, e, g, x, y, d, ring=True):
    for r in range(n):
        here, before = pl.ds(8 + 8 * r, 8), pl.ds(7 + 8 * r, 8)
        south = [y[t, here, :] for t in range(tiles)]
        south_prev = lane_prev(south, ring)
        for t in range(tiles):
            flow = (x[t, here, :] - x[t, before, :]) + (south[t] - south_prev[t])
            eta = e[t, here, :] - flow
            wet = jnp.maximum(d[t, here, :] + eta, 0.0)
            e[t, here, :] = eta
            g[t, here, :] = wet
            if r == 0:
                e[t, pl.ds(8 + 8 * n, 8), :] = eta
                g[t, pl.ds(8 + 8 * n, 8), :] = wet


def flux_pass(tiles, n, e, g, x, y, kx, ky, ox, oy, fix, ring=True, ghost=True):
    for r in range(n):
        here, after = pl.ds(8 + 8 * r, 8), pl.ds(9 + 8 * r, 8)
        eta = [e[t, here, :] for t in range(tiles)]
        wet = [g[t, here, :] for t in range(tiles)]
        eta_next, wet_next = lane_next(eta, ring), lane_next(wet, ring)
        for t in range(tiles):
            fx = new_flux(
                x[t, here, :], eta[t], e[t, after, :], wet[t], g[t, after, :], ox[t, here, :], kx[t, here, :]
            )
            fx = fix(r, t, fx)
            x[t, here, :] = fx
            if ghost and r == n - 1:
                x[t, pl.ds(0, 8), :] = fx
            y[t, here, :] = new_flux(
                y[t, here, :], eta[t], eta_next[t], wet[t], wet_next[t], oy[t, here, :], ky[t, here, :]
            )


def pieces(value):
    high = value.astype(jnp.bfloat16)
    rest = value - high.astype(F32)
    middle = rest.astype(jnp.bfloat16)
    return high, middle, (rest - middle.astype(F32)).astype(jnp.bfloat16)


def dot(a, b):
    return lax.dot_general(a, b, (((1,), (0,)), ((), ())), preferred_element_type=F32)


def pick_columns(value, picks):
    rows = value.shape[0]
    result = dot(jnp.concatenate(pieces(value), 0), picks.astype(jnp.bfloat16))
    return (result[2 * rows :] + result[rows : 2 * rows]) + result[:rows]


def pick_rows(picks, value):
    cols = value.shape[1]
    result = dot(picks.astype(jnp.bfloat16), jnp.concatenate(pieces(value), 1))
    return (result[:, 2 * cols :] + result[:, cols : 2 * cols]) + result[:, :cols]


def iota(shape, dim):
    return lax.broadcasted_iota(jnp.int32, shape, dim)


def place_of(block_size):
    gx = lax.axis_index("gx")
    slot = lax.rem(gx, block_size)
    return gx, lax.div(gx, block_size), slot == 0, slot == block_size - 1


def edge_rows(load, own_offset, ocean_rows):
    west, east = load(own_offset - 1), load(ocean_rows - 1)
    return jnp.concatenate([west, east] + [east] * 14, 0)


def grid_edges(sources, spread_to, wf, rows, edges):
    spread = pick_columns(jnp.concatenate(sources, 1), spread_to.astype(F32))
    for t in range(edges.shape[1]):
        cut = spread[:, t * LANES : (t + 1) * LANES]
        wet_first = wf[t, pl.ds(8, 8), :]
        wet_last = wf[t, pl.ds(rows, 8), :]
        edges[0, t, :, :] = jnp.broadcast_to(cut[0:1, :] * wet_first[0:1, :], (8, LANES))
        edges[1, t, :, :] = jnp.broadcast_to(cut[1:2, :] * wet_last[7:8, :], (8, LANES))


def run_coastal(tiles, n, rows, first, last, state, edges, ring, unroll):
    e, g, x, y, d, kx, ky, ox, oy = state
    sub = iota((8, LANES), 0)
    ghost = n > rows // 8
    west_mask = (sub == 7) & first
    east_mask = (sub == 7) & last

    def fix(r, t, fx):
        if r == rows // 8 - 1:
            fx = jnp.where(east_mask, edges[1, t, :, :], fx)
        if ghost and r == n - 1:
            fx = jnp.where(west_mask, edges[0, t, :, :], fx)
        return fx

    for t in range(tiles):
        before = x[t, pl.ds(8 * n, 8), :] if ghost else 0.0
        x[t, pl.ds(0, 8), :] = jnp.where(west_mask, edges[0, t, :, :], before)

    def step(_, carry):
        level_pass(tiles, n, e, g, x, y, d, ring)
        flux_pass(tiles, n, e, g, x, y, kx, ky, ox, oy, fix, ring, ghost)
        return carry

    lax.fori_loop(0, FSTEPS, step, 0, unroll=unroll)


def interior_kernel(block_size, *refs):
    table, offsets, fine, ocean = refs[0], refs[1], refs[2:8], refs[8:13]
    outs, (even_out, odd_out, strip) = refs[13:16], refs[16:19]
    e, g, x, y, d, kf, wf, kx, ky, ox, oy, edges = refs[19:]
    ocean_mx = ocean[1]
    ocean_rows = ocean_mx.shape[0]
    rows, cols = fine[0].shape
    tiles = cols // LANES
    n = rows // 8
    gx, grid, first, last = place_of(block_size)
    dest = (e, x, y, d, kf, wf)
    for r in range(n):
        src, here = pl.ds(8 * r, 8), pl.ds(8 + 8 * r, 8)
        values = [fine_fields(fine, src, pl.ds(t * LANES, LANES), table) for t in range(tiles)]
        for t in range(tiles):
            for f in range(6):
                dest[f][t, here, :] = values[t][f]
        ocean_values = ocean_fields(ocean, src, pl.ds(0, LANES), table) if 8 * r < ocean_rows else ()
        even_out[src, :], odd_out[src, :] = packed_columns(columns_parts(values[0], values[-1], ocean_values))
        for f in range(6):
            strip[f, src, :] = strip_lanes(values[0][f], values[-1][f])

    spread_to = iota((LANES, cols), 0) == lax.div(iota((LANES, cols), 1), R)
    sources = [edge_rows(lambda at: ocean_mx[pl.ds(at, 1), :] * SB, offsets[grid], ocean_rows)]
    grid_edges(sources, spread_to, wf, rows, edges)
    prepare_faces(tiles, n, kf, wf, kx, ky, ox, oy, False)
    run_coastal(tiles, n, rows, first, last, (e, g, x, y, d, kx, ky, ox, oy), edges, False, 6)
    for r in range(n):
        to, here = pl.ds(8 * r, 8), pl.ds(8 + 8 * r, 8)
        for t in range(tiles):
            at_cols = pl.ds(t * LANES, LANES)
            outs[0][to, at_cols] = e[t, here, :] * (1.0 / SA)
            outs[1][to, at_cols] = x[t, here, :] * (1.0 / SB)
            outs[2][to, at_cols] = y[t, here, :] * (1.0 / SB)


def rows_kernel(block_size, *refs):
    table, offsets, fine = refs[0], refs[1], refs[2:8]
    pairs_only = block_size == 2
    count = 1 if pairs_only else 2
    messages = refs[8 : 8 + count]
    inner = refs[8 + count : 11 + count]
    outs, out_means = refs[11 + count : 14 + count], refs[14 + count]
    e, g, x, y, d, kf, wf, kx, ky, ox, oy = refs[15 + count :]
    rows, cols = fine[0].shape
    ocean_rows = out_means.shape[0]
    tiles = cols // LANES
    near = 2 * REACH // 8
    n = near + HALO // 8
    gx, grid, first, last = place_of(block_size)
    gx_is_even = lax.rem(gx, 2) == 0
    sub = iota((8, LANES), 0)
    dest = (e, x, y, d, kf, wf)
    for i in range(3):
        outs[i][...] = inner[i][...]

    for side in range(count):
        to_next = gx_is_even if pairs_only else side == 0
        start = jnp.where(to_next, rows - 8 * near, 0) if pairs_only else (rows - 8 * near) * (side == 0)
        for r in range(near):
            src = pl.ds(pl.multiple_of(start + 8 * r, 8), 8) if pairs_only else pl.ds(start + 8 * r, 8)
            for t in range(tiles):
                for f, value in enumerate(fine_fields(fine, src, pl.ds(t * LANES, LANES), table)):
                    dest[f][t, pl.ds(8 + 8 * r, 8), :] = value
        for f in range(6):
            for t in range(tiles):
                block = halo_blocks(pairs_only, messages, f * tiles + t, gx_is_even)[side]
                dest[f][t, pl.ds(8 + 8 * near, HALO), :] = block
        prepare_faces(tiles, n, kf, wf, kx, ky, ox, oy, False)
        for t in range(tiles):
            x[t, pl.ds(0, 8), :] = x[t, pl.ds(8 * n, 8), :]

        def step(_, carry):
            level_pass(tiles, n, e, g, x, y, d, False)
            flux_pass(tiles, n, e, g, x, y, kx, ky, ox, oy, lambda r, t, fx: fx, False)
            return carry

        lax.fori_loop(0, FSTEPS, step, 0, unroll=FSTEPS)

        open_end = jnp.logical_not(jnp.where(to_next, last, first))
        for half in range(2):
            if pairs_only:
                src = pl.multiple_of(jnp.where(to_next, 8 * (near - 2 + half), 8 * half), 8)
                to = pl.multiple_of(jnp.where(to_next, rows - HALO + 8 * half, 8 * half), 8)
            else:
                src = 8 * (near - 2 + half) if to_next else 8 * half
                to = rows - HALO + 8 * half if to_next else 8 * half
            depth_in = jnp.where(to_next, HALO - 1 - (sub + 8 * half), sub + 8 * half)
            take = (depth_in < FSTEPS) & open_end
            for i, (held, scale) in enumerate(((e, 1.0 / SA), (x, 1.0 / SB), (y, 1.0 / SB))):
                for t in range(tiles):
                    at_cols = pl.ds(t * LANES, LANES)
                    value = held[t, pl.ds(8 + src, 8), :] * scale
                    outs[i][pl.ds(to, 8), at_cols] = jnp.where(take, value, outs[i][pl.ds(to, 8), at_cols])

    gather_cols = (lax.div(iota((cols, LANES), 0), R) == iota((cols, LANES), 1)).astype(F32)
    out_means[...] = coarse_means(outs[0][...], gather_cols, offsets[grid], ocean_rows)


def coarse_means(eta, gather_cols, own_offset, ocean_rows):
    shape = (ocean_rows, eta.shape[0])
    coarse_row = lax.rem(lax.div(iota(shape, 1), R) + own_offset, ocean_rows)
    gather_rows = (coarse_row == iota(shape, 0)).astype(F32)
    return pick_rows(gather_rows, pick_columns(eta, gather_cols)) * (1.0 / (R * R))


def border_kernel(block_size, cols, *refs):
    pairs_only = block_size == 2
    count = 1 if pairs_only else 2
    offsets, strip, ocean_mx, messages = refs[0], refs[1], refs[2], refs[3 : 3 + count]
    gy_even, gy_odd, ocean_odd, inner_means = refs[3 + count : 7 + count]
    outs, out_even, out_odd = refs[7 + count : 10 + count], refs[10 + count], refs[11 + count]
    e, g, x, y, d, kf, wf, kx, ky, ox, oy, edges = refs[12 + count :]
    rows = strip.shape[1]
    own = cols // LANES
    n = rows // 8 + (HALO // 8) * (1 if pairs_only else 2)
    gx, grid, first, last = place_of(block_size)
    gx_is_even = lax.rem(gx, 2) == 0
    gy_is_even = lax.rem(lax.axis_index("gy"), 2) == 0
    lane = iota((8, LANES), 1)
    dest = (e, x, y, d, kf, wf)
    halos = [
        [halo_blocks(pairs_only, messages, f * own + t, gx_is_even) for t in (0, own - 1)] for f in range(6)
    ]
    for r in range(n):
        src, here = pl.ds(8 * r, 8), pl.ds(8 + 8 * r, 8)
        if 8 * r < rows:
            mine = [strip[f, src, :] for f in range(6)]
        else:
            side, half = divmod(r - rows // 8, HALO // 8)
            cut = slice(8 * half, 8 * half + 8)
            mine = [strip_lanes(halos[f][0][side][cut], halos[f][1][side][cut]) for f in range(6)]
        from_even, from_odd = gy_even[src, :], gy_odd[src, :]
        from_east = jnp.where(gy_is_even, from_even, from_odd)
        from_west = jnp.where(gy_is_even, from_odd, from_even)
        for f in range(6):
            east = roll_to(from_east, 16 * f, 64)
            west = roll_to(from_west, 16 * f, LANES - 16)
            value = jnp.where((lane >= 64) & (lane < 80), east, mine[f])
            dest[f][0, here, :] = jnp.where(lane < LANES - 16, value, west)

    ocean_rows = ocean_mx.shape[0]
    from_even = edge_rows(lambda at: gy_even[pl.ds(at, 1), :], offsets[grid], ocean_rows)
    from_odd = edge_rows(lambda at: gy_odd[pl.ds(at, 1), :], offsets[grid], ocean_rows)
    from_east = jnp.where(gy_is_even, from_even, from_odd)
    from_west = jnp.where(gy_is_even, from_odd, from_even)
    mx_halo = jnp.where(
        iota((16, LANES), 1) < ITERS,
        roll_to(from_east, OLANE + ITERS, 0),
        roll_to(from_west, OLANE + ITERS, LANES - ITERS),
    )
    to = iota((2 * LANES, LANES), 1)
    wanted = jnp.where(to < 32, lax.div(to, R), lax.div(to + (cols - 64), R))
    wanted = jnp.where(to < 64, wanted, jnp.where(to < 80, LANES + lax.div(to - 64, R), 0))
    wanted = jnp.where(to < LANES - 16, wanted, 2 * LANES - 1 - lax.div(LANES - 1 - to, R))
    spread_to = iota((2 * LANES, LANES), 0) == wanted
    own_rows = edge_rows(lambda at: ocean_mx[pl.ds(at, 1), :] * SB, offsets[grid], ocean_rows)
    grid_edges([own_rows, mx_halo], spread_to, wf, rows, edges)
    prepare_faces(1, n, kf, wf, kx, ky, ox, oy)
    run_coastal(1, n, rows, first, last, (e, g, x, y, d, kx, ky, ox, oy), edges, True, FSTEPS)

    for i, (held, scale) in enumerate(((e, 1.0 / SA), (x, 1.0 / SB), (y, 1.0 / SB))):
        outs[i][...] = held[0, 8 : 8 + rows, :] * scale
    source, target = iota((LANES, LANES), 0), iota((LANES, LANES), 1)
    column = jnp.where(source < 32, source, source + (cols - 64))
    inside = (source < FSTEPS) | ((source >= 64 - FSTEPS) & (source < 64))
    gather = ((lax.div(column, R) == target) & inside).astype(F32)
    means = coarse_means(outs[0][...], gather, offsets[grid], ocean_rows)
    col = iota((ocean_rows, LANES), 1)
    means = jnp.where((col < ITERS) | (col >= LANES - ITERS), means, inner_means[...])
    out_even[...] = means
    out_odd[0:ocean_rows, :] = means
    out_odd[ocean_rows : ocean_rows + 5 * ITERS, :] = ocean_odd[...]
    for k, side in enumerate((gy_even, gy_odd)):
        corner = jnp.where(gx_is_even, side[0:ITERS, :], side[ocean_rows - ITERS : ocean_rows, :])
        out_odd[pl.ds(ocean_rows + (5 + k) * ITERS, ITERS), :] = corner


def finish_kernel(*refs):
    inner, strips, table, ocean = refs[0:3], refs[3:6], refs[6], refs[7:12]
    gy_even, gy_odd, gx_even = refs[12:15]
    outs, state, final, sems = refs[15:18], refs[18], refs[19], refs[20]
    rows, cols = final.shape[1:]
    own = cols // LANES
    lane = iota((8, LANES), 1)
    copies = [pltpu.make_async_copy(final.at[i], outs[i], sems.at[i]) for i in range(3)]
    for i in range(3):
        for r in range(rows // 8):
            to = pl.ds(8 * r, 8)
            value = strips[i][to, :]
            for t in range(own):
                at_cols = pl.ds(t * LANES, LANES)
                kept = inner[i][to, at_cols]
                if t == 0:
                    kept = jnp.where(lane < FSTEPS, value, kept)
                if t == own - 1:
                    kept = jnp.where(lane >= LANES - FSTEPS, roll_to(value, 32, LANES - 32), kept)
                final[i, to, at_cols] = kept
        copies[i].start()

    ocean_rows = ocean[0].shape[0]
    gx_is_even = lax.rem(lax.axis_index("gx"), 2) == 0
    for r in range(ocean_rows // 8):
        src = pl.ds(8 * r, 8)
        for j, value in enumerate(ocean_fields(ocean, src, pl.ds(0, LANES), table)):
            state[j, 0, src, :] = value
            state[j, 1, src, :] = unpack_ocean(gy_even[src, :], gy_odd[src, :], j)
    halo = pl.ds(ocean_rows, 8)
    gap = jnp.zeros((ITERS, LANES), F32)
    for j in range(5):
        state[j, 0, halo, :] = ocean_halo(ocean_part(gx_even, j), gap, gx_is_even)
        state[j, 1, halo, :] = unpack_ocean(gy_even[halo, :], gy_odd[halo, :], j)
    for copy in copies:
        copy.wait()


def unpack_ocean(from_even, from_odd, j):
    gy_is_even = lax.rem(lax.axis_index("gy"), 2) == 0
    lane = iota((8, LANES), 1)
    from_east = jnp.where(gy_is_even, from_even, from_odd)
    from_west = jnp.where(gy_is_even, from_odd, from_even)
    east = roll_to(from_east, OLANE + ITERS * j, 0)
    west = roll_to(from_west, OLANE + ITERS * j, LANES - ITERS)
    return jnp.where(lane < ITERS, east, jnp.where(lane >= LANES - ITERS, west, 0.0))


def ocean_kernel(block_size, *refs):
    offsets, state, rolled, got_even, got_odd = refs[:5]
    out_eta, out_x, out_y = refs[5:8]
    e, g, x, y, d, kf, kx, ky, ox, oy = refs[8:]
    rows, cols = out_eta.shape
    tiles = 2
    n = rows // 8 + 1
    gx, gy = lax.axis_index("gx"), lax.axis_index("gy")
    gx_is_even = lax.rem(gx, 2) == 0
    lane = iota((8, LANES), 1)
    sub = iota((8, LANES), 0)
    here = pl.ds(8 + rows, 8)
    gap = jnp.zeros((ITERS, LANES), F32)
    corners = [got_odd[pl.ds(rows + (5 + k) * ITERS, ITERS), :] for k in range(2)]
    corners = [ocean_halo(gap, corner, gx_is_even) for corner in corners]
    for j, field in enumerate((e, x, y, d, kf)):
        for t in range(tiles):
            field[t, 8 : 8 + rows + 8, :] = state[j, t]
        odd = ocean_halo(gap, got_odd[pl.ds(rows + j * ITERS, ITERS), :], gx_is_even)
        field[0, here, :] = field[0, here, :] + odd
        field[1, here, :] = field[1, here, :] + unpack_ocean(*corners, j)

    prepare_faces(tiles, n, kf, None, kx, ky, None, None)
    rows_total, cols_total = rows * lax.axis_size("gx"), cols * lax.axis_size("gy")
    for r in range(n):
        here = pl.ds(8 + 8 * r, 8)
        row = sub + 8 * r
        row = jnp.where(row >= rows + 4, row - (rows + 8), row) + gx * rows
        for t in range(tiles):
            col = lane if t == 0 else jnp.where(lane < 64, lane + LANES, lane - LANES)
            col = col + gy * cols
            ox[t, here, :] = jnp.where((row >= 0) & (row < rows_total - 1), 1.0, CLOSED)
            oy[t, here, :] = jnp.where((col >= 0) & (col < cols_total - 1), 1.0, CLOSED)
    for t in range(tiles):
        x[t, pl.ds(0, 8), :] = x[t, pl.ds(8 * n, 8), :]

    def step(_, carry):
        level_pass(tiles, n, e, g, x, y, d)
        flux_pass(tiles, n, e, g, x, y, kx, ky, ox, oy, lambda r, t, fx: fx)
        return carry

    lax.fori_loop(0, ITERS, step, 0, unroll=4)
    _, grid, _, _ = place_of(block_size)
    own_offset = offsets[grid]
    left_offset = jnp.where(gx >= 1, offsets[lax.div(jnp.maximum(gx - 1, 0), block_size)], 0)
    for r in range(rows // 8):
        to, here = pl.ds(8 * r, 8), pl.ds(8 + 8 * r, 8)
        row = sub + 8 * r
        arrived = jnp.where(gx_is_even, got_odd[to, :], got_even[to, :])
        level = jnp.where(row < left_offset, arrived, e[0, here, :] * (1.0 / SA))
        out_eta[to, :] = jnp.where(row >= own_offset, rolled[to, :], level)
        out_x[to, :] = x[0, here, :] * (1.0 / SB)
        out_y[to, :] = y[0, here, :] * (1.0 / SB)


def shape(*dims):
    return jax.ShapeDtypeStruct(dims, F32)


def params():
    return pltpu.CompilerParams(vmem_limit_bytes=48 * 1024 * 1024)


def shards(
    ocean_eta,
    ocean_mx,
    ocean_ny,
    ocean_depth,
    ocean_class,
    manning,
    fine_eta,
    fine_qx,
    fine_qy,
    fine_depth,
    fine_wet,
    fine_class,
    fine_offset,
):
    ocean_rows, ocean_cols = ocean_eta.shape
    rows, cols = fine_eta.shape
    own = cols // LANES
    gx_count = lax.axis_size("gx")
    block_size = min(16, gx_count // 2)
    pairs_only = block_size == 2
    fine = (fine_eta, fine_qx, fine_qy, fine_depth, fine_wet, fine_class)
    ocean = (ocean_eta, ocean_mx, ocean_ny, ocean_depth, ocean_class)

    def vmem(*dims, dtype=F32):
        return pltpu.VMEM(dims, dtype)

    count = 1 if pairs_only else 2
    fine_length, ocean_length = 6 * own * REACH, 5 * ITERS
    lengths = [fine_length + ocean_length, fine_length][:count] + [ocean_length]
    *gx_fine, ocean_odd = pl.pallas_call(
        functools.partial(pack_rows_kernel, pairs_only),
        out_shape=tuple(shape(length, LANES) for length in lengths),
        in_specs=[SMEM] + [ANY] * 11,
        out_specs=(VMEM,) * len(lengths),
        scratch_shapes=[
            vmem(4, count, HALO, cols),
            vmem(2, count, HALO, cols, dtype=jnp.int32),
            vmem(4, ocean_rows, ocean_cols),
            vmem(ocean_rows, ocean_cols, dtype=jnp.int32),
            pltpu.SemaphoreType.DMA((6 * count + 5,)),
        ],
        name="pack_rows",
    )(manning, *fine, *ocean)
    gx_fine = [swap(message, "gx") for swap, message in zip((swap_even, swap_odd), gx_fine)]

    *inner, own_even, own_odd, strip = pl.pallas_call(
        functools.partial(interior_kernel, block_size),
        out_shape=(shape(rows, cols),) * 3 + (shape(rows, LANES),) * 2 + (shape(6, rows, LANES),),
        in_specs=[SMEM, SMEM] + [VMEM] * 11,
        out_specs=(VMEM,) * 6,
        scratch_shapes=[vmem(own, rows + 16, LANES)] * 11 + [vmem(2, own, 8, LANES)],
        compiler_params=params(),
        cost_estimate=pl.CostEstimate(flops=0, bytes_accessed=20_000_000, transcendentals=0),
        name="interior",
    )(manning, fine_offset, *fine, *ocean)

    n = rows // 8 + (HALO // 8) * count
    gy_even, gy_odd = pl.pallas_call(
        functools.partial(pack_columns_kernel, pairs_only, own, ocean_rows),
        out_shape=(shape(8 * n, LANES),) * 2,
        in_specs=[VMEM] * (2 + count),
        out_specs=(VMEM,) * 2,
        compiler_params=params(),
        name="pack_columns",
    )(own_even, own_odd, *gx_fine)
    gy_even = swap_even(gy_even, "gy")
    gy_odd = swap_odd(gy_odd, "gy")

    *inner, means = pl.pallas_call(
        functools.partial(rows_kernel, block_size),
        out_shape=(shape(rows, cols),) * 3 + (shape(ocean_rows, ocean_cols),),
        in_specs=[SMEM, SMEM] + [VMEM] * (9 + count),
        out_specs=(VMEM,) * 4,
        scratch_shapes=[vmem(own, 2 * REACH + HALO + 16, LANES)] * 11,
        compiler_params=params(),
        cost_estimate=pl.CostEstimate(flops=0, bytes_accessed=10_000_000, transcendentals=0),
        name="rows",
    )(manning, fine_offset, *fine, *gx_fine, *inner)

    odd_length = ocean_rows + 7 * ITERS
    *strips, rolled, to_odd = pl.pallas_call(
        functools.partial(border_kernel, block_size, cols),
        out_shape=(shape(rows, LANES),) * 3 + (shape(ocean_rows, ocean_cols), shape(odd_length, LANES)),
        in_specs=[SMEM] + [VMEM] * (6 + count),
        out_specs=(VMEM,) * 5,
        scratch_shapes=[vmem(1, 8 * n + 16, LANES)] * 11 + [vmem(2, 1, 8, LANES)],
        compiler_params=params(),
        name="border",
    )(fine_offset, strip, ocean_mx, *gx_fine, gy_even, gy_odd, ocean_odd, means)
    got_even = swap_even(rolled, "gx")
    got_odd = swap_odd(to_odd, "gx")

    n = ocean_rows // 8 + 1
    feta, fqx, fqy, state = pl.pallas_call(
        finish_kernel,
        out_shape=(shape(rows, cols),) * 3 + (shape(5, 2, 8 * n, LANES),),
        in_specs=[VMEM] * 6 + [SMEM] + [VMEM] * 8,
        out_specs=(ANY,) * 3 + (VMEM,),
        scratch_shapes=[vmem(3, rows, cols), pltpu.SemaphoreType.DMA((3,))],
        compiler_params=params(),
        cost_estimate=pl.CostEstimate(flops=0, bytes_accessed=5_000_000, transcendentals=0),
        name="finish",
    )(*inner, *strips, manning, *ocean, gy_even, gy_odd, gx_fine[0])

    eta, mx, ny = pl.pallas_call(
        functools.partial(ocean_kernel, block_size),
        out_shape=(shape(ocean_rows, ocean_cols),) * 3,
        in_specs=[SMEM] + [VMEM] * 4,
        out_specs=(VMEM,) * 3,
        scratch_shapes=[vmem(2, 8 * n + 16, LANES)] * 10,
        compiler_params=params(),
        name="ocean",
    )(fine_offset, state, rolled, got_even, got_odd)
    return (eta, mx, ny, feta, fqx, fqy)


def solution(mesh):
    tile = P(("scen", "gx"), "gy")
    in_specs = (tile,) * 5 + (P(),) + (tile,) * 6 + (P("scen"),)
    return jax.shard_map(shards, mesh=mesh, in_specs=in_specs, out_specs=(tile,) * 6, check_vma=False)
```
